128 devices in a mesh: dp: 8 (over x, core), vocab: 16 (over z, y).
Axes of the slice: x: 4, y: 4, z: 4, core: 2. Of those that a mesh axis runs over, the one named last changes fastest.
Arguments:
- hidden: bfloat16 [2048, 7168], P('dp'), may hold values from -6 to 6
- head_weight: bfloat16 [7168, 8192], P('dp', 'vocab'), may hold values from -0.0625 to 0.0625
- proj_mid: bfloat16 [7168, 1792], P('dp', 'vocab'), may hold values from -0.0625 to 0.0625
- proj_tail: bfloat16 [7168, 448], P('dp', 'vocab'), may hold values from -0.0625 to 0.0625
- mid_weight: bfloat16 [1792, 20480], P('dp', 'vocab'), may hold values from -0.125 to 0.125
- tail_weight: bfloat16 [448, 36864], P('dp', 'vocab'), may hold values from -0.25 to 0.25
- target_head: bfloat16 [2048, 8192], P('dp', 'vocab'), may hold values from -20 to 420
- target_mid: bfloat16 [2048, 20480], P('dp', 'vocab'), may hold values from -20 to 420
- target_tail: bfloat16 [2048, 36864], P('dp', 'vocab'), may hold values from -20 to 420
- top_ids: int32 [2048], P('dp'), may hold values from 0 to 65535
- tier_of: int32 [65536], replicated, may hold values from 0 to 65535, each once
Outputs:
- head_grad: bfloat16 [7168, 8192], P('dp', 'vocab')
- proj_mid_grad: bfloat16 [7168, 1792], P('dp', 'vocab')
- proj_tail_grad: bfloat16 [7168, 448], P('dp', 'vocab')
- mid_grad: bfloat16 [1792, 20480], P('dp', 'vocab')
- tail_grad: bfloat16 [448, 36864], P('dp', 'vocab')
- hidden_grad: bfloat16 [2048, 7168], P('dp', 'vocab')
- row_loss: float32 [2048], P('dp')
The draws below stay inside these ranges and needn't reach their ends.
Inputs may be any that keep to these rules, and one draw needn't show every extreme that they name: `tier_of`: ids below 8192 in tier order are the head tier, then 20480 of the middle tier, then the last tier.
All inputs are finite; a program needn't handle non-finite values.
Results may differ from the reference program's by a relative error of at most 0.03.
Values may be sent and summed in bfloat16 or wider, within the bound.
No kernel may reach another device: no remote copies, remote signals or barrier semaphores. Data moves between devices by JAX's collectives and lax.ppermute only.
A program may use at most 128 MiB of HBM per device.

```python
import math
import jax
import jax.numpy as jnp
import numpy as np
from jax import lax

D = 7168
V0 = 8192
V1 = 20480
V2 = 36864
R1 = 1792
R2 = 448
TOK_DEV = 256
TOKENS = 2048
V = 65536
N_DP = 8
N_VOCAB = 16


def normal_rows(key, width):
    return jnp.clip(3.0 * jax.random.normal(key, (TOKENS, width), jnp.float32), -18.0, 18.0)


def draw_target_head(key, part):
    key = jax.random.fold_in(key, 1)
    return normal_rows(key, V0).astype(jnp.bfloat16)


def draw_target_mid(key, part):
    key = jax.random.fold_in(key, 2)
    return normal_rows(key, V1).astype(jnp.bfloat16)


def draw_target_tail(key, part):
    key = jax.random.fold_in(key, 3)
    return normal_rows(key, V2).astype(jnp.bfloat16)


def place_ends(entries, own_key, least, high):
    extent = entries.shape
    spot = [jax.random.randint(jax.random.fold_in(own_key, axis), (), 0, extent[axis]) for axis in range(len(extent))]
    entries = entries.at[tuple(spot)].set(least)
    longest = extent.index(max(extent))
    spot[longest] = (spot[longest] + 1) % extent[longest]
    return entries.at[tuple(spot)].set(high)


def block_scale(own_key, extent, pieces, smallest, largest):
    def one(position, blocks):
        heights = jax.random.uniform(jax.random.fold_in(jax.random.fold_in(own_key, 6), position), (blocks,), jnp.float32, smallest / len(pieces), largest / len(pieces))
        return jnp.repeat(jnp.exp(heights), extent[position] // blocks).reshape((-1,) + (1,) * (len(extent) - position - 1))

    gain = one(*pieces[0])
    for cut in pieces[1:]:
        gain = gain * one(*cut)
    return gain


def rank_table(amount, skew):
    portions = [(1 << 20) // math.isqrt(standing ** skew) + 1 for standing in range(1, amount + 1)]
    scale = 1 + sum(portions) // (1 << 30)
    return np.cumsum(np.array([max(1, weight // scale) for weight in portions]))


def skewed_ids(key, shape, amount, slope):
    table = rank_table(amount, slope)
    pick = jax.random.randint(jax.random.fold_in(key, 1), shape, 0, int(table[amount - 1]))
    standing = jnp.searchsorted(jnp.asarray(table, jnp.int32), pick, side="right")
    return jax.random.permutation(jax.random.fold_in(key, 2), amount)[standing].astype(jnp.int32)


def noise(own_key, extent, scale, bound, pieces=(), held_as=jnp.bfloat16):
    drawn = scale * jax.random.normal(own_key, extent, jnp.float32)
    if pieces:
        drawn = drawn * block_scale(own_key, extent, pieces, -0.22, 0.18)
    return jnp.clip(drawn, -bound, bound).astype(held_as)


def setup_inputs(seed: int = 0) -> dict:
    arg_keys = jax.random.split(jax.random.key(seed), 12)
    return {
        "hidden": noise(arg_keys[0], (TOKENS, D), 1.0, 6.0, ((0, 8),)),
        "head_weight": noise(arg_keys[1], (D, V0), D ** -0.5, 0.0625, ((0, 8), (1, 16))),
        "proj_mid": noise(arg_keys[2], (D, R1), D ** -0.5, 0.0625, ((0, 8), (1, 16))),
        "proj_tail": noise(arg_keys[3], (D, R2), D ** -0.5, 0.0625, ((0, 8), (1, 16))),
        "mid_weight": noise(arg_keys[4], (R1, V1), R1 ** -0.5, 0.125, ((0, 8), (1, 16))),
        "tail_weight": noise(arg_keys[5], (R2, V2), R2 ** -0.5, 0.25, ((0, 8), (1, 16))),
        "target_head": draw_target_head(jax.random.fold_in(arg_keys[11], 71), 0),
        "target_mid": draw_target_mid(jax.random.fold_in(arg_keys[11], 71), 0),
        "target_tail": draw_target_tail(jax.random.fold_in(arg_keys[11], 71), 0),
        "top_ids": place_ends(skewed_ids(arg_keys[9], (TOKENS,), V, 2), jax.random.fold_in(arg_keys[9], 3), 0, V - 1).astype(jnp.int32),
        "tier_of": jax.random.permutation(arg_keys[10], V).astype(jnp.int32),
    }


def rounded(quantity):
    return lax.optimization_barrier(quantity.astype(jnp.bfloat16)).astype(jnp.float32)


def contract(left, right):
    return lax.dot_general(left, right, (((0,), (0,)), ((), ())), preferred_element_type=jnp.float32)


def shard_partials(gradient, weight):
    left = gradient.reshape(gradient.shape[0], N_VOCAB, -1).astype(jnp.float32)
    right = weight.reshape(weight.shape[0], N_VOCAB, -1).astype(jnp.float32)
    partials = jnp.einsum("rvc,kvc->vrk", left, right)
    return jnp.sum(rounded(partials), axis=0)


def tier_gradients(logits, targets, positions, offsets):
    hit_masks = [positions[:, None] == (offset + jnp.arange(block.shape[1], dtype=jnp.int32))[None, :] for block, offset in zip(logits, offsets)]
    top_draft = jnp.max(jnp.stack([jnp.max(block, axis=1) for block in logits]), axis=0)
    top_teacher = jnp.max(jnp.stack([jnp.max(block, axis=1) for block in targets]), axis=0)
    mass_draft = sum(jnp.sum(jnp.exp(block - top_draft[:, None]), axis=1) for block in logits)
    mass_teacher = sum(jnp.sum(jnp.exp(block - top_teacher[:, None]), axis=1) for block in targets)
    cross = sum(jnp.sum(jnp.exp(teach - top_teacher[:, None]) * (teach - draft), axis=1) for draft, teach in zip(logits, targets))
    picked = sum(jnp.sum(jnp.where(mask, draft, 0.0), axis=1) for draft, mask in zip(logits, hit_masks))
    lse_draft = top_draft + jnp.log(mass_draft)
    lse_teacher = top_teacher + jnp.log(mass_teacher)
    row_loss = cross / mass_teacher - lse_teacher + 2.0 * lse_draft - picked
    grads = tuple((2.0 * jnp.exp(draft - lse_draft[:, None]) - jnp.exp(teach - lse_teacher[:, None]) - jnp.where(mask, 1.0, 0.0)).astype(jnp.bfloat16) for draft, teach, mask in zip(logits, targets, hit_masks))
    return grads, row_loss


def reference(hidden, head_weight, proj_mid, proj_tail, mid_weight, tail_weight, target_head, target_mid, target_tail, top_ids, tier_of):
    positions_all = jnp.take(tier_of, top_ids).astype(jnp.int32)
    offsets = (0, V0, V0 + V1)
    head_cols = V0 // N_VOCAB
    mid_ranks = R1 // N_VOCAB
    tail_ranks = R2 // N_VOCAB

    def group_step(carried, group_index):
        first_row = (group_index * TOK_DEV).astype(jnp.int32)

        def take_rows(source):
            return lax.dynamic_slice_in_dim(source, first_row, TOK_DEV, 0)

        block_hidden = take_rows(hidden)
        z_mid = jnp.dot(block_hidden, proj_mid, preferred_element_type=jnp.float32).astype(jnp.bfloat16)
        z_tail = jnp.dot(block_hidden, proj_tail, preferred_element_type=jnp.float32).astype(jnp.bfloat16)
        logits = (jnp.dot(block_hidden, head_weight, preferred_element_type=jnp.float32),
                  jnp.dot(z_mid, mid_weight, preferred_element_type=jnp.float32),
                  jnp.dot(z_tail, tail_weight, preferred_element_type=jnp.float32))
        targets = tuple(take_rows(source).astype(jnp.float32) for source in (target_head, target_mid, target_tail))
        grads, row_loss = tier_gradients(logits, targets, take_rows(positions_all), offsets)
        g_head, g_mid, g_tail = grads
        dz_mid = shard_partials(g_mid, mid_weight).astype(jnp.bfloat16)
        dz_tail = shard_partials(g_tail, tail_weight).astype(jnp.bfloat16)

        def shard_step(running, shard_index):
            head_part = jnp.dot(lax.dynamic_slice_in_dim(g_head, shard_index * head_cols, head_cols, 1),
                                lax.dynamic_slice_in_dim(head_weight, shard_index * head_cols, head_cols, 1).T,
                                preferred_element_type=jnp.float32)
            mid_part = jnp.dot(lax.dynamic_slice_in_dim(dz_mid, shard_index * mid_ranks, mid_ranks, 1),
                               lax.dynamic_slice_in_dim(proj_mid, shard_index * mid_ranks, mid_ranks, 1).T,
                               preferred_element_type=jnp.float32)
            tail_part = jnp.dot(lax.dynamic_slice_in_dim(dz_tail, shard_index * tail_ranks, tail_ranks, 1),
                                lax.dynamic_slice_in_dim(proj_tail, shard_index * tail_ranks, tail_ranks, 1).T,
                                preferred_element_type=jnp.float32)
            return running + rounded(head_part + mid_part + tail_part), None

        hidden_total, _ = lax.scan(shard_step, jnp.zeros((TOK_DEV, D), jnp.float32), jnp.arange(N_VOCAB, dtype=jnp.int32))
        head_acc, mid_acc, tail_acc, pmid_acc, ptail_acc = carried
        head_acc = head_acc + rounded(contract(block_hidden, g_head))
        mid_acc = mid_acc + rounded(contract(z_mid, g_mid))
        tail_acc = tail_acc + rounded(contract(z_tail, g_tail))
        pmid_acc = pmid_acc + rounded(contract(block_hidden, dz_mid))
        ptail_acc = ptail_acc + rounded(contract(block_hidden, dz_tail))
        return (head_acc, mid_acc, tail_acc, pmid_acc, ptail_acc), (hidden_total.astype(jnp.bfloat16), row_loss)

    start_acc = (jnp.zeros((D, V0), jnp.float32), jnp.zeros((R1, V1), jnp.float32), jnp.zeros((R2, V2), jnp.float32),
                 jnp.zeros((D, R1), jnp.float32), jnp.zeros((D, R2), jnp.float32))
    totals, outputs = lax.scan(group_step, start_acc, jnp.arange(N_DP, dtype=jnp.int32))
    hidden_blocks, loss_blocks = outputs
    return (totals[0].astype(jnp.bfloat16), totals[3].astype(jnp.bfloat16), totals[4].astype(jnp.bfloat16),
            totals[1].astype(jnp.bfloat16), totals[2].astype(jnp.bfloat16),
            hidden_blocks.reshape(TOKENS, D), loss_blocks.reshape(TOKENS))
```

```python
import jax
import jax.numpy as jnp
from jax import lax
from jax.sharding import PartitionSpec as P

BF16 = jnp.bfloat16
F32 = jnp.float32


def dot(left, right, left_dim, right_dim):
    return lax.dot_general(
        left, right, (((left_dim,), (right_dim,)), ((), ())), preferred_element_type=F32
    )


def swap(block, flip):
    return lax.ppermute(block, "dp", [(i, i ^ flip) for i in range(lax.axis_size("dp"))])


def gather_dp(block):
    half = block.shape[0] // 2
    near = swap(block, 2)
    other = swap(block, 6)
    far = jnp.concatenate([swap(other[:half], 2), swap(near[half:], 6)], axis=0)
    me = lax.axis_index("dp")
    out = jnp.zeros((lax.axis_size("dp"),) + block.shape, block.dtype)
    for flip, part in ((0, block), (2, near), (6, other), (4, far)):
        out = lax.dynamic_update_index_in_dim(out, part, me ^ flip, 0)
        out = lax.dynamic_update_index_in_dim(out, swap(part, 1), me ^ flip ^ 1, 0)
    return out


def spread_vocab(block):
    size = lax.axis_size("vocab")
    return lax.all_to_all(jnp.broadcast_to(block[None], (size,) + block.shape), "vocab", 0, 0)


def per_device(
    hidden,
    head_weight,
    proj_mid,
    proj_tail,
    mid_weight,
    tail_weight,
    target_head,
    target_mid,
    target_tail,
    top_ids,
    tier_of,
):
    n_vocab = lax.axis_size("vocab")
    n_dp = lax.axis_size("dp")
    v = lax.axis_index("vocab")
    rows, width = hidden.shape
    depth = head_weight.shape[0]
    rank_mid, rank_tail = proj_mid.shape[1], proj_tail.shape[1]
    ranks = rank_mid + rank_tail

    with jax.named_scope("gather_proj"):
        proj_t = jnp.concatenate([proj_mid.T, proj_tail.T], axis=0)
        proj_all = gather_dp(proj_t.T)
        proj_full = proj_all.reshape(width, ranks)
    with jax.named_scope("gather_mid_tail"):
        mid_full = lax.all_gather(mid_weight, "dp", axis=0, tiled=True)
        tail_full = lax.all_gather(tail_weight, "dp", axis=0, tiled=True)
    with jax.named_scope("codes"):
        codes = dot(proj_full, hidden, 0, 1).astype(BF16)
    with jax.named_scope("spread_codes"):
        codes_all = spread_vocab(codes)
        z_mid = codes_all[:, :rank_mid].reshape(n_vocab * rank_mid, rows)
        z_tail = codes_all[:, rank_mid:].reshape(n_vocab * rank_tail, rows)
    with jax.named_scope("gather_head"):
        head_full = gather_dp(head_weight).reshape(width, -1)
    with jax.named_scope("spread_hidden"):
        piece = rows // n_vocab
        mine = lax.dynamic_slice_in_dim(hidden, v * piece, piece, 0)
        mine = mine.reshape(piece, n_dp, depth).transpose(1, 0, 2)
        mine = lax.all_to_all(mine, "dp", 0, 0)
        x_all = spread_vocab(mine)
        x_all = x_all.transpose(1, 0, 2, 3).reshape(n_dp * rows, depth)

    with jax.named_scope("logits"):
        logits = (
            dot(hidden, head_full, 1, 0),
            dot(z_mid, mid_full, 0, 0),
            dot(z_tail, tail_full, 0, 0),
        )
    with jax.named_scope("statistics"):
        targets = (target_head.astype(F32), target_mid.astype(F32), target_tail.astype(F32))
        widths = (head_weight.shape[1], mid_weight.shape[1], tail_weight.shape[1])
        starts = (0, widths[0] * n_vocab, (widths[0] + widths[1]) * n_vocab)
        positions = jnp.take(tier_of, top_ids)
        hits = [
            positions[:, None] == (start + v * w + jnp.arange(w, dtype=jnp.int32))[None, :]
            for start, w in zip(starts, widths)
        ]

        def top(blocks):
            return jnp.max(jnp.stack([jnp.max(block, axis=1) for block in blocks]), axis=0)

        near_s, near_t = top(logits), top(targets)
        mass_s = sum(jnp.sum(jnp.exp(s - near_s[:, None]), axis=1) for s in logits)
        mass_t = sum(jnp.sum(jnp.exp(t - near_t[:, None]), axis=1) for t in targets)
        cross = sum(
            jnp.sum(jnp.exp(t - near_t[:, None]) * (t - s), axis=1)
            for s, t in zip(logits, targets)
        )
        picked = sum(
            jnp.sum(jnp.where(hit, s, 0.0), axis=1) for s, hit in zip(logits, hits)
        )
        zero = jnp.zeros_like(picked)
        packed = jnp.stack([near_s, near_t, mass_s, mass_t, cross, picked, zero, zero])
    with jax.named_scope("spread_statistics"):
        packed = spread_vocab(packed)
        near_s, near_t, mass_s, mass_t, cross, picked = (packed[:, k] for k in range(6))
        top_s, top_t = jnp.max(near_s, axis=0), jnp.max(near_t, axis=0)
        scale_s, scale_t = jnp.exp(near_s - top_s[None]), jnp.exp(near_t - top_t[None])
        mass_s = jnp.sum(mass_s * scale_s, axis=0)
        mass_t = jnp.sum(mass_t * scale_t, axis=0)
        cross = jnp.sum(cross * scale_t, axis=0)
        picked = jnp.sum(picked, axis=0)
        lse_s = top_s + jnp.log(mass_s)
        lse_t = top_t + jnp.log(mass_t)
        row_loss = cross / mass_t - lse_t + 2.0 * lse_s - picked
    with jax.named_scope("grad_logits"):
        g_head, g_mid, g_tail = tuple(
            (
                2.0 * jnp.exp(s - lse_s[:, None])
                - jnp.exp(t - lse_t[:, None])
                - jnp.where(hit, 1.0, 0.0)
            ).astype(BF16)
            for s, t, hit in zip(logits, targets, hits)
        )

    with jax.named_scope("code_grads"):
        dz = jnp.concatenate(
            [
                dot(mid_full, g_mid, 1, 1).astype(BF16).reshape(n_vocab, rank_mid, rows),
                dot(tail_full, g_tail, 1, 1).astype(BF16).reshape(n_vocab, rank_tail, rows),
            ],
            axis=1,
        )
        dz = lax.all_to_all(dz, "vocab", 0, 0)
        dz = jnp.sum(dz.astype(F32), axis=0).astype(BF16)
    with jax.named_scope("mid_tail_grads"):
        mid_grad = lax.psum_scatter(
            dot(z_mid, g_mid, 1, 0).astype(BF16), "dp", scatter_dimension=0, tiled=True
        )
        tail_grad = lax.psum_scatter(
            dot(z_tail, g_tail, 1, 0).astype(BF16), "dp", scatter_dimension=0, tiled=True
        )
    with jax.named_scope("hidden_grad"):
        term = dot(head_full, g_head, 1, 1) + dot(proj_full, dz, 1, 0)
        term = term.astype(BF16).reshape(n_vocab, width // n_vocab, rows)
        term = lax.all_to_all(term, "vocab", 0, 0)
        hidden_grad = jnp.sum(term.astype(F32), axis=0).astype(BF16).T
    with jax.named_scope("head_proj_grads"):
        g_all = gather_dp(g_head).reshape(n_dp * rows, -1)
        head_grad = dot(x_all, g_all, 0, 0).astype(BF16)
        dz_all = gather_dp(dz.T).reshape(n_dp * rows, ranks)
        proj_grad = dot(x_all, dz_all, 0, 0).astype(BF16)
    return (
        head_grad,
        proj_grad[:, :rank_mid],
        proj_grad[:, rank_mid:],
        mid_grad,
        tail_grad,
        hidden_grad,
        row_loss,
    )


def solution(mesh):
    split = P("dp", "vocab")
    in_specs = (P("dp", None),) + (split,) * 8 + (P("dp"), P())
    out_specs = (split,) * 6 + (P("dp"),)
    return jax.shard_map(
        per_device, mesh=mesh, in_specs=in_specs, out_specs=out_specs, check_vma=False
    )
```

```python
import functools

import jax
import jax.numpy as jnp
from jax import lax
from jax.experimental import pallas as pl
from jax.experimental.pallas import tpu as pltpu
from jax.sharding import PartitionSpec as P

BF16 = jnp.bfloat16
F32 = jnp.float32


def dot(left, right, left_dim, right_dim):
    return lax.dot_general(
        left, right, (((left_dim,), (right_dim,)), ((), ())), preferred_element_type=F32
    )


def swap(block, flip):
    return lax.ppermute(block, "dp", [(i, i ^ flip) for i in range(lax.axis_size("dp"))])


def place_kernel(axis, me_ref, *refs):
    blocks, out, sems = refs[:-2], refs[-2], refs[-1]
    copies = []
    for flip, block in enumerate(blocks):
        size = block.shape[axis]
        start = pl.multiple_of((me_ref[0] ^ flip) * size, size)
        spot = out.at[pl.ds(start, size)] if axis == 0 else out.at[:, pl.ds(start, size)]
        copies.append(pltpu.make_async_copy(block, spot, sems.at[flip]))
    for copy in copies:
        copy.start()
    for copy in copies:
        copy.wait()


def place(blocks, axis):
    shape = list(blocks[0].shape)
    shape[axis] *= len(blocks)
    moved = 2 * len(blocks) * blocks[0].size * blocks[0].dtype.itemsize
    return pl.pallas_call(
        functools.partial(place_kernel, axis),
        out_shape=jax.ShapeDtypeStruct(tuple(shape), blocks[0].dtype),
        in_specs=[pl.BlockSpec(memory_space=pltpu.SMEM)]
        + [pl.BlockSpec(memory_space=pltpu.VMEM)] * len(blocks),
        out_specs=pl.BlockSpec(memory_space=pl.ANY),
        scratch_shapes=[pltpu.SemaphoreType.DMA((len(blocks),))],
        compiler_params=pltpu.CompilerParams(vmem_limit_bytes=16 << 20),
        cost_estimate=pl.CostEstimate(flops=0, bytes_accessed=moved, transcendentals=0),
    )(lax.axis_index("dp").astype(jnp.int32).reshape(1), *blocks)


def gather_dp(block, axis):
    half = block.shape[0] // 32 * 16
    near = swap(block, 2)
    other = swap(block, 6)
    far = jnp.concatenate([swap(other[:half], 2), swap(near[half:], 6)], axis=0)
    parts = [block, near, far, other]
    return place([p for part in parts for p in (part, swap(part, 1))], axis)


def spread_vocab(block):
    size = lax.axis_size("vocab")
    return lax.all_to_all(jnp.broadcast_to(block[None], (size,) + block.shape), "vocab", 0, 0)


def per_device(
    hidden,
    head_weight,
    proj_mid,
    proj_tail,
    mid_weight,
    tail_weight,
    target_head,
    target_mid,
    target_tail,
    top_ids,
    tier_of,
):
    n_vocab = lax.axis_size("vocab")
    n_dp = lax.axis_size("dp")
    v = lax.axis_index("vocab")
    rows, width = hidden.shape
    depth = head_weight.shape[0]
    rank_mid, rank_tail = proj_mid.shape[1], proj_tail.shape[1]
    ranks = rank_mid + rank_tail

    with jax.named_scope("gather_proj"):
        pad = -ranks % 16
        proj_t = jnp.concatenate(
            [proj_mid.T, proj_tail.T, jnp.zeros((pad, depth), BF16)], axis=0
        )
        proj_full = gather_dp(proj_t, 1)
    with jax.named_scope("gather_mid_tail"):
        mid_full = lax.all_gather(mid_weight, "dp", axis=0, tiled=True)
        tail_full = lax.all_gather(tail_weight, "dp", axis=0, tiled=True)
    with jax.named_scope("codes"):
        codes = dot(proj_full, hidden, 1, 1).astype(BF16)
    with jax.named_scope("spread_codes"):
        codes_all = spread_vocab(codes)
        z_mid = codes_all[:, :rank_mid].reshape(n_vocab * rank_mid, rows)
        z_tail = codes_all[:, rank_mid:ranks].reshape(n_vocab * rank_tail, rows)
    with jax.named_scope("gather_head"):
        head_full = gather_dp(head_weight, 0)
    with jax.named_scope("spread_hidden"):
        piece = rows // n_vocab
        mine = lax.dynamic_slice_in_dim(hidden, v * piece, piece, 0)
        mine = mine.reshape(piece, n_dp, depth).transpose(1, 0, 2)
        mine = lax.all_to_all(mine, "dp", 0, 0)
        x_all = spread_vocab(mine)
        x_all = x_all.transpose(1, 0, 2, 3).reshape(n_dp * rows, depth)

    with jax.named_scope("logits"):
        logits = (
            dot(hidden, head_full, 1, 0),
            dot(z_mid, mid_full, 0, 0),
            dot(z_tail, tail_full, 0, 0),
        )
    with jax.named_scope("statistics"):
        targets = (target_head.astype(F32), target_mid.astype(F32), target_tail.astype(F32))
        widths = (head_weight.shape[1], mid_weight.shape[1], tail_weight.shape[1])
        starts = (0, widths[0] * n_vocab, (widths[0] + widths[1]) * n_vocab)
        positions = jnp.take(tier_of, top_ids)
        hits = [
            positions[:, None] == (start + v * w + jnp.arange(w, dtype=jnp.int32))[None, :]
            for start, w in zip(starts, widths)
        ]

        def top(blocks):
            return jnp.max(jnp.stack([jnp.max(block, axis=1) for block in blocks]), axis=0)

        near_s, near_t = top(logits), top(targets)
        mass_s = sum(jnp.sum(jnp.exp(s - near_s[:, None]), axis=1) for s in logits)
        mass_t = sum(jnp.sum(jnp.exp(t - near_t[:, None]), axis=1) for t in targets)
        cross = sum(
            jnp.sum(jnp.exp(t - near_t[:, None]) * (t - s), axis=1)
            for s, t in zip(logits, targets)
        )
        picked = sum(
            jnp.sum(jnp.where(hit, s, 0.0), axis=1) for s, hit in zip(logits, hits)
        )
        zero = jnp.zeros_like(picked)
        packed = jnp.stack([near_s, near_t, mass_s, mass_t, cross, picked, zero, zero])
    with jax.named_scope("spread_statistics"):
        packed, x_all = lax.optimization_barrier((packed, x_all))
        packed = spread_vocab(packed)
        near_s, near_t, mass_s, mass_t, cross, picked = (packed[:, k] for k in range(6))
        top_s, top_t = jnp.max(near_s, axis=0), jnp.max(near_t, axis=0)
        scale_s, scale_t = jnp.exp(near_s - top_s[None]), jnp.exp(near_t - top_t[None])
        mass_s = jnp.sum(mass_s * scale_s, axis=0)
        mass_t = jnp.sum(mass_t * scale_t, axis=0)
        cross = jnp.sum(cross * scale_t, axis=0)
        picked = jnp.sum(picked, axis=0)
        lse_s = top_s + jnp.log(mass_s)
        lse_t = top_t + jnp.log(mass_t)
        row_loss = cross / mass_t - lse_t + 2.0 * lse_s - picked
    with jax.named_scope("grad_logits"):
        g_head, g_mid, g_tail = tuple(
            (
                2.0 * jnp.exp(s - lse_s[:, None])
                - jnp.exp(t - lse_t[:, None])
                - jnp.where(hit, 1.0, 0.0)
            ).astype(BF16)
            for s, t, hit in zip(logits, targets, hits)
        )

    with jax.named_scope("code_grads"):
        dz = jnp.concatenate(
            [
                dot(mid_full, g_mid, 1, 1).astype(BF16).reshape(n_vocab, rank_mid, rows),
                dot(tail_full, g_tail, 1, 1).astype(BF16).reshape(n_vocab, rank_tail, rows),
                jnp.zeros((n_vocab, pad, rows), BF16),
            ],
            axis=1,
        )
        dz = lax.all_to_all(dz, "vocab", 0, 0)
        dz = jnp.sum(dz.astype(F32), axis=0).astype(BF16)
    with jax.named_scope("mid_tail_grads"):
        mid_grad = lax.psum_scatter(
            dot(z_mid, g_mid, 1, 0).astype(BF16), "dp", scatter_dimension=0, tiled=True
        )
        tail_grad = lax.psum_scatter(
            dot(z_tail, g_tail, 1, 0).astype(BF16), "dp", scatter_dimension=0, tiled=True
        )
    with jax.named_scope("hidden_grad"):
        term = dot(head_full, g_head, 1, 1) + dot(proj_full, dz, 0, 0)
        term = term.astype(BF16).reshape(n_vocab, width // n_vocab, rows)
        term = lax.all_to_all(term, "vocab", 0, 0)
        hidden_grad = jnp.sum(term.astype(F32), axis=0).astype(BF16).T
    with jax.named_scope("head_proj_grads"):
        g_all = gather_dp(g_head, 0)
        head_grad = dot(x_all, g_all, 0, 0).astype(BF16)
        dz_all = gather_dp(dz, 1)
        proj_grad = dot(x_all, dz_all, 0, 1).astype(BF16)
    return (
        head_grad,
        proj_grad[:, :rank_mid],
        proj_grad[:, rank_mid:ranks],
        mid_grad,
        tail_grad,
        hidden_grad,
        row_loss,
    )


def solution(mesh):
    split = P("dp", "vocab")
    in_specs = (P("dp", None),) + (split,) * 8 + (P("dp"), P())
    out_specs = (split,) * 6 + (P("dp"),)
    return jax.shard_map(
        per_device, mesh=mesh, in_specs=in_specs, out_specs=out_specs, check_vma=False
    )
```

```python
import functools

import jax
import jax.numpy as jnp
from jax import lax
from jax.experimental import pallas as pl
from jax.experimental.pallas import tpu as pltpu
from jax.sharding import PartitionSpec as P

BF16 = jnp.bfloat16
F32 = jnp.float32


def dot(left, right, left_dim, right_dim):
    return lax.dot_general(
        left, right, (((left_dim,), (right_dim,)), ((), ())), preferred_element_type=F32
    )


def swap(block, axis_name, flip):
    pairs = [(i, i ^ flip) for i in range(lax.axis_size(axis_name))]
    return lax.ppermute(block, axis_name, pairs)


def ring_near(block, axis_name, step):
    return swap(block, axis_name, step), swap(block, axis_name, 3 * step)


def ring_far(near, other, axis_name, step, half):
    return jnp.concatenate(
        [swap(other[:half], axis_name, step), swap(near[half:], axis_name, 3 * step)], axis=0
    )


def place_kernel(axis, spots_ref, *refs):
    blocks, out, sems = refs[:-2], refs[-2], refs[-1]
    copies = []
    for k, block in enumerate(blocks):
        size = block.shape[axis]
        start = pl.multiple_of(spots_ref[k] * size, size)
        spot = out.at[(slice(None),) * axis + (pl.ds(start, size),)]
        copies.append(pltpu.make_async_copy(block, spot, sems.at[k]))
    for copy in copies:
        copy.start()
    for copy in copies:
        copy.wait()


def place(blocks, spots, axis):
    shape = list(blocks[0].shape)
    shape[axis] *= len(blocks)
    moved = 2 * len(blocks) * blocks[0].size * blocks[0].dtype.itemsize
    return pl.pallas_call(
        functools.partial(place_kernel, axis),
        out_shape=jax.ShapeDtypeStruct(tuple(shape), blocks[0].dtype),
        in_specs=[pl.BlockSpec(memory_space=pltpu.SMEM)]
        + [pl.BlockSpec(memory_space=pltpu.VMEM)] * len(blocks),
        out_specs=pl.BlockSpec(memory_space=pl.ANY),
        scratch_shapes=[pltpu.SemaphoreType.DMA((len(blocks),))],
        compiler_params=pltpu.CompilerParams(vmem_limit_bytes=16 << 20),
        cost_estimate=pl.CostEstimate(flops=0, bytes_accessed=moved, transcendentals=0),
    )(jnp.stack(spots).astype(jnp.int32), *blocks)


def half_rows(block):
    return block.shape[0] // 32 * 16


def both_cores(parts, axis):
    blocks = [p for part in parts for p in (part, swap(part, "dp", 1))]
    me = lax.axis_index("dp")
    return place(blocks, [me ^ flip for flip in range(len(blocks))], axis)


def gather_dp(block, axis):
    near, other = ring_near(block, "dp", 2)
    far = ring_far(near, other, "dp", 2, half_rows(block))
    return both_cores([block, near, far, other], axis)


def in_vmem(kernel, out_shape, *operands):
    outs = out_shape if isinstance(out_shape, tuple) else (out_shape,)
    size = sum(a.size * a.dtype.itemsize for a in operands + outs)
    return pl.pallas_call(
        kernel,
        out_shape=out_shape,
        compiler_params=pltpu.CompilerParams(vmem_limit_bytes=32 << 20),
        cost_estimate=pl.CostEstimate(flops=2 * 10**9, bytes_accessed=size, transcendentals=0),
    )(*operands)


def columns(width_mid, width_tail, quarters):
    spans = [(q * width_mid, width_mid) for q in range(quarters)]
    return spans + [(quarters * width_mid, width_tail)]


def logits_kernel(spans, z_ref, w_ref, mid_ref, tail_ref):
    mid = None
    for q, (start, size) in enumerate(spans):
        part = dot(z_ref[q], w_ref[:, start : start + size], 0, 0)
        if q == len(spans) - 1:
            tail_ref[...] = part
        else:
            mid = part if mid is None else mid + part
    mid_ref[...] = mid


def code_grads_kernel(spans, w_ref, mid_ref, tail_ref, out_ref):
    for q, (start, size) in enumerate(spans):
        grad = tail_ref if q == len(spans) - 1 else mid_ref
        out_ref[q] = dot(w_ref[:, start : start + size], grad[...], 1, 1).astype(BF16)


def weight_grads_kernel(spans, z_ref, mid_ref, tail_ref, out_ref):
    for q, (start, size) in enumerate(spans):
        grad = tail_ref if q == len(spans) - 1 else mid_ref
        out_ref[:, start : start + size] = dot(z_ref[q], grad[...], 1, 0).astype(BF16)


def spread_vocab(block):
    size = lax.axis_size("vocab")
    return lax.all_to_all(jnp.broadcast_to(block[None], (size,) + block.shape), "vocab", 0, 0)


def per_device(
    hidden,
    head_weight,
    proj_mid,
    proj_tail,
    mid_weight,
    tail_weight,
    target_head,
    target_mid,
    target_tail,
    top_ids,
    tier_of,
):
    n_vocab = lax.axis_size("vocab")
    n_dp = lax.axis_size("dp")
    v = lax.axis_index("vocab")
    rows, width = hidden.shape
    depth = head_weight.shape[0]
    rank_mid, rank_tail = proj_mid.shape[1], proj_tail.shape[1]
    ranks = rank_mid + rank_tail

    with jax.named_scope("gather_proj"):
        pad = -ranks % 16
        proj_t = jnp.concatenate(
            [proj_mid.T, proj_tail.T, jnp.zeros((pad, depth), BF16)], axis=0
        )
        proj_full = gather_dp(proj_t, 1)
    with jax.named_scope("gather_mid_tail"):
        depth_tail, quarters = tail_weight.shape[0], mid_weight.shape[0] // tail_weight.shape[0]
        spans = columns(mid_weight.shape[1], tail_weight.shape[1], quarters)
        packed_weight = jnp.concatenate(
            [mid_weight[q * depth_tail : (q + 1) * depth_tail] for q in range(quarters)]
            + [tail_weight],
            axis=1,
        )
        packed_full = lax.all_gather(packed_weight, "dp", axis=0, tiled=True)
    with jax.named_scope("gather_head_near"):
        head_near, head_other = ring_near(head_weight, "dp", 2)
    with jax.named_scope("spread_hidden"):
        piece = rows // n_vocab
        mine = lax.dynamic_slice_in_dim(hidden, v * piece, piece, 0)
        mine = mine.reshape(piece, n_dp, depth).transpose(1, 0, 2)
        mine = lax.all_to_all(mine, "dp", 0, 0)
        mine, packed_full = lax.optimization_barrier((mine, packed_full))
        x_all = lax.all_gather(mine.reshape(n_dp * piece, depth), "vocab", axis=0)
        x_all = x_all.reshape(n_vocab, n_dp, piece, depth).transpose(1, 0, 2, 3)
        x_all = x_all.reshape(n_dp * rows, depth)
    with jax.named_scope("codes"):
        codes = dot(proj_full, hidden, 1, 1).astype(BF16)
        codes, head_near, head_other = lax.optimization_barrier((codes, head_near, head_other))
    with jax.named_scope("gather_head_far"):
        head_far = ring_far(head_near, head_other, "dp", 2, half_rows(head_weight))
    with jax.named_scope("spread_codes"):
        codes_all = spread_vocab(codes)
        by_dp = codes_all.reshape(n_dp, n_vocab // n_dp, ranks + pad, rows)
        per = rank_mid // depth_tail
        z = [
            by_dp[:, q // per, (q % per) * depth_tail : (q % per + 1) * depth_tail]
            for q in range(quarters)
        ] + [by_dp[:, :, rank_mid:ranks].reshape(n_dp, depth_tail, rows)]
        z = jnp.stack(z).reshape(quarters + 1, n_dp * depth_tail, rows)
    with jax.named_scope("gather_head"):
        head_full = both_cores([head_weight, head_near, head_far, head_other], 0)

    with jax.named_scope("logits"):
        mid_logits, tail_logits = in_vmem(
            functools.partial(logits_kernel, spans),
            (
                jax.ShapeDtypeStruct((rows, mid_weight.shape[1]), F32),
                jax.ShapeDtypeStruct((rows, tail_weight.shape[1]), F32),
            ),
            z,
            packed_full,
        )
        logits = (dot(hidden, head_full, 1, 0), mid_logits, tail_logits)
    with jax.named_scope("statistics"):
        targets = (target_head.astype(F32), target_mid.astype(F32), target_tail.astype(F32))
        widths = (head_weight.shape[1], mid_weight.shape[1], tail_weight.shape[1])
        starts = (0, widths[0] * n_vocab, (widths[0] + widths[1]) * n_vocab)
        positions = jnp.take(tier_of, top_ids)
        hits = [
            positions[:, None] == (start + v * w + jnp.arange(w, dtype=jnp.int32))[None, :]
            for start, w in zip(starts, widths)
        ]

        def top(blocks):
            return jnp.max(jnp.stack([jnp.max(block, axis=1) for block in blocks]), axis=0)

        near_s, near_t = top(logits), top(targets)
        mass_s = sum(jnp.sum(jnp.exp(s - near_s[:, None]), axis=1) for s in logits)
        mass_t = sum(jnp.sum(jnp.exp(t - near_t[:, None]), axis=1) for t in targets)
        cross = sum(
            jnp.sum(jnp.exp(t - near_t[:, None]) * (t - s), axis=1)
            for s, t in zip(logits, targets)
        )
        picked = sum(
            jnp.sum(jnp.where(hit, s, 0.0), axis=1) for s, hit in zip(logits, hits)
        )
        zero = jnp.zeros_like(picked)
        packed = jnp.stack([near_s, near_t, mass_s, mass_t, cross, picked, zero, zero])
    with jax.named_scope("spread_statistics"):
        packed = spread_vocab(packed)
        near_s, near_t, mass_s, mass_t, cross, picked = (packed[:, k] for k in range(6))
        top_s, top_t = jnp.max(near_s, axis=0), jnp.max(near_t, axis=0)
        scale_s, scale_t = jnp.exp(near_s - top_s[None]), jnp.exp(near_t - top_t[None])
        mass_s = jnp.sum(mass_s * scale_s, axis=0)
        mass_t = jnp.sum(mass_t * scale_t, axis=0)
        cross = jnp.sum(cross * scale_t, axis=0)
        picked = jnp.sum(picked, axis=0)
        lse_s = top_s + jnp.log(mass_s)
        lse_t = top_t + jnp.log(mass_t)
        row_loss = cross / mass_t - lse_t + 2.0 * lse_s - picked
    with jax.named_scope("grad_logits"):
        g_head, g_mid, g_tail = tuple(
            (
                2.0 * jnp.exp(s - lse_s[:, None])
                - jnp.exp(t - lse_t[:, None])
                - jnp.where(hit, 1.0, 0.0)
            ).astype(BF16)
            for s, t, hit in zip(logits, targets, hits)
        )

    with jax.named_scope("code_grads"):
        dz = in_vmem(
            functools.partial(code_grads_kernel, spans),
            jax.ShapeDtypeStruct(z.shape, BF16),
            packed_full,
            g_mid,
            g_tail,
        ).reshape(quarters + 1, n_dp, depth_tail, rows)
        dz = jnp.concatenate(
            [
                dz[:quarters].transpose(1, 0, 2, 3).reshape(n_vocab, rank_mid, rows),
                dz[quarters].reshape(n_vocab, rank_tail, rows),
                jnp.zeros((n_vocab, pad, rows), BF16),
            ],
            axis=1,
        )
        dz, g_mid = lax.optimization_barrier((dz, g_mid))
        dz = lax.all_to_all(dz, "vocab", 0, 0)
        dz = jnp.sum(dz.astype(F32), axis=0).astype(BF16)
    with jax.named_scope("mid_tail_grads"):
        packed_grad = in_vmem(
            functools.partial(weight_grads_kernel, spans),
            jax.ShapeDtypeStruct(packed_full.shape, BF16),
            z,
            g_mid,
            g_tail,
        )
        packed_grad = lax.psum_scatter(packed_grad, "dp", scatter_dimension=0, tiled=True)
        pieces = [packed_grad[:, start : start + size] for start, size in spans]
        mid_grad = jnp.concatenate(pieces[:quarters], axis=0)
        tail_grad = pieces[quarters]
    with jax.named_scope("hidden_grad"):
        term = dot(head_full, g_head, 1, 1) + dot(proj_full, dz, 0, 0)
        term = term.astype(BF16).reshape(n_vocab, width // n_vocab, rows)
        term = lax.all_to_all(term, "vocab", 0, 0)
    with jax.named_scope("head_proj_grads"):
        g_all = gather_dp(g_head, 0)
        head_grad = dot(x_all, g_all, 0, 0).astype(BF16)
        dz_all = gather_dp(dz, 1)
        proj_grad = dot(x_all, dz_all, 0, 1).astype(BF16)
    with jax.named_scope("hidden_grad_sum"):
        term, head_grad, proj_grad = lax.optimization_barrier((term, head_grad, proj_grad))
        hidden_grad = jnp.sum(term.astype(F32), axis=0).astype(BF16).T
    return (
        head_grad,
        proj_grad[:, :rank_mid],
        proj_grad[:, rank_mid:ranks],
        mid_grad,
        tail_grad,
        hidden_grad,
        row_loss,
    )


def solution(mesh):
    split = P("dp", "vocab")
    in_specs = (P("dp", None),) + (split,) * 8 + (P("dp"), P())
    out_specs = (split,) * 6 + (P("dp"),)
    return jax.shard_map(
        per_device, mesh=mesh, in_specs=in_specs, out_specs=out_specs, check_vma=False
    )
```

```python
import functools

import jax
import jax.numpy as jnp
from jax import lax
from jax.experimental import pallas as pl
from jax.experimental.pallas import tpu as pltpu
from jax.sharding import PartitionSpec as P

BF16 = jnp.bfloat16
F32 = jnp.float32


def dot(left, right, left_dim, right_dim):
    return lax.dot_general(
        left, right, (((left_dim,), (right_dim,)), ((), ())), preferred_element_type=F32
    )


def swap(block, axis_name, flip):
    pairs = [(i, i ^ flip) for i in range(lax.axis_size(axis_name))]
    return lax.ppermute(block, axis_name, pairs)


def ring_near(block, axis_name, step):
    return swap(block, axis_name, step), swap(block, axis_name, 3 * step)


def ring_far(near, other, axis_name, step, half):
    return jnp.concatenate(
        [swap(other[:half], axis_name, step), swap(near[half:], axis_name, 3 * step)], axis=0
    )


def place_kernel(axis, spots_ref, *refs):
    blocks, out, sems = refs[:-2], refs[-2], refs[-1]
    copies = []
    for k, block in enumerate(blocks):
        size = block.shape[axis]
        start = pl.multiple_of(spots_ref[k] * size, size)
        spot = out.at[(slice(None),) * axis + (pl.ds(start, size),)]
        copies.append(pltpu.make_async_copy(block, spot, sems.at[k]))
    for copy in copies:
        copy.start()
    for copy in copies:
        copy.wait()


def place(blocks, spots, axis, hidden_flops=0):
    shape = list(blocks[0].shape)
    shape[axis] *= len(blocks)
    moved = 2 * len(blocks) * blocks[0].size * blocks[0].dtype.itemsize
    return pl.pallas_call(
        functools.partial(place_kernel, axis),
        out_shape=jax.ShapeDtypeStruct(tuple(shape), blocks[0].dtype),
        in_specs=[pl.BlockSpec(memory_space=pltpu.SMEM)]
        + [pl.BlockSpec(memory_space=pltpu.VMEM)] * len(blocks),
        out_specs=pl.BlockSpec(memory_space=pl.ANY),
        scratch_shapes=[pltpu.SemaphoreType.DMA((len(blocks),))],
        compiler_params=pltpu.CompilerParams(vmem_limit_bytes=16 << 20),
        cost_estimate=pl.CostEstimate(flops=hidden_flops, bytes_accessed=moved, transcendentals=0),
    )(jnp.stack(spots).astype(jnp.int32), *blocks)


def half_rows(block):
    return block.shape[0] // 32 * 16


def both_cores(parts, axis, hidden_flops=0):
    blocks = [p for part in parts for p in (part, swap(part, "dp", 1))]
    me = lax.axis_index("dp")
    return place(blocks, [me ^ flip for flip in range(len(blocks))], axis, hidden_flops)


def gather_dp(block, axis, hidden_flops=0):
    near, other = ring_near(block, "dp", 2)
    far = ring_far(near, other, "dp", 2, half_rows(block))
    return both_cores([block, near, far, other], axis, hidden_flops)


def in_vmem(kernel, out_shape, *operands, in_specs=None, scratch_shapes=()):
    outs = out_shape if isinstance(out_shape, tuple) else (out_shape,)
    size = sum(a.size * a.dtype.itemsize for a in operands + outs)
    specs = in_specs or [pl.BlockSpec(memory_space=pltpu.VMEM)] * len(operands)
    return pl.pallas_call(
        kernel,
        out_shape=out_shape,
        in_specs=specs,
        scratch_shapes=scratch_shapes,
        compiler_params=pltpu.CompilerParams(vmem_limit_bytes=48 << 20),
        cost_estimate=pl.CostEstimate(flops=2 * 10**9, bytes_accessed=size, transcendentals=0),
    )(*operands)


def fetch(source, held, sems, spans, base=0):
    copies = [
        pltpu.make_async_copy(
            source.at[:, pl.ds(start, size)], held.at[:, pl.ds(start - base, size)], sems.at[k]
        )
        for k, (start, size) in enumerate(spans)
    ]
    for copy in copies:
        copy.start()
    return copies


def column_spans(groups, widths):
    spans, start = [], 0
    for count, width in zip(groups, widths):
        for _ in range(count):
            spans.append((start, width))
            start += width
    return spans


def pack_kernel(spans, quarters, mid_ref, tail_ref, head_ref, out_ref):
    depth = tail_ref.shape[0]
    mid, head = mid_ref[...].astype(F32), head_ref[...].astype(F32)
    for k, (start, size) in enumerate(spans):
        if k < quarters:
            piece = mid[k * depth : (k + 1) * depth].astype(BF16)
        elif k == quarters:
            piece = tail_ref[...]
        else:
            row = (k - quarters - 1) * depth
            piece = head[row : row + depth].astype(BF16)
        out_ref[:, start : start + size] = piece


def unpack_kernel(spans, packed_ref, mid_ref, tail_ref):
    quarters = [packed_ref[:, a : a + size].astype(F32) for a, size in spans[:-1]]
    mid_ref[...] = jnp.concatenate(quarters, axis=0).astype(BF16)
    start, size = spans[-1]
    tail_ref[...] = packed_ref[:, start : start + size]


ROWS = 16


def row_blocks(rows, body):
    def step(k, carry):
        body(pl.ds(pl.multiple_of(k * ROWS, ROWS), ROWS))
        return carry

    lax.fori_loop(0, rows // ROWS, step, 0)


def hits_of(base, position, shape):
    return position - base == lax.broadcasted_iota(jnp.int32, shape, 1)


def forward_kernel(
    spans, quarters, ranks, bases_ref, w_any, codes_ref, hidden_ref, position_ref,
    target_head, target_mid, target_tail,
    z_ref, head_ref, mid_ref, tail_ref, stats_ref, w_ref, sems,
):
    copies = fetch(w_any, w_ref, sems, spans)
    rank_mid, rank_tail = ranks
    n_dp, per = 2 * codes_ref.shape[0] // quarters, quarters // 2
    depth = rank_mid // per
    codes = [codes_ref[k].astype(F32) for k in range(codes_ref.shape[0])]
    for q in range(quarters):
        first = q % per * depth
        z_ref[q] = jnp.concatenate(
            [codes[2 * j + q // per][first : first + depth] for j in range(n_dp)], axis=0
        ).astype(BF16)
    z_ref[quarters] = jnp.concatenate(
        [code[rank_mid : rank_mid + rank_tail] for code in codes], axis=0
    ).astype(BF16)
    for k, (start, size) in enumerate(spans):
        copies[k].wait()
        weight = w_ref[:, start : start + size]
        if k < quarters:
            part = dot(z_ref[k], weight, 0, 0)
            mid_ref[...] = part if k == 0 else mid_ref[...] + part
        elif k == quarters:
            tail_ref[...] = dot(z_ref[k], weight, 0, 0)
        else:
            part = dot(hidden_ref[k - quarters - 1], weight, 0, 0)
            head_ref[...] = part if k == quarters + 1 else head_ref[...] + part

    tiers = ((head_ref, target_head), (mid_ref, target_mid), (tail_ref, target_tail))

    def body(block):
        pairs = [(s[block, :], t[block, :].astype(F32)) for s, t in tiers]
        position = position_ref[block, :]
        top_s = top_t = None
        for s, t in pairs:
            here_s, here_t = (jnp.max(a, axis=1, keepdims=True) for a in (s, t))
            top_s = here_s if top_s is None else jnp.maximum(top_s, here_s)
            top_t = here_t if top_t is None else jnp.maximum(top_t, here_t)
        mass_s = mass_t = cross = picked = jnp.zeros_like(top_s)
        for k, (s, t) in enumerate(pairs):
            hit = hits_of(bases_ref[k], position, s.shape)
            weight = jnp.exp(t - top_t)
            mass_s += jnp.sum(jnp.exp(s - top_s), axis=1, keepdims=True)
            mass_t += jnp.sum(weight, axis=1, keepdims=True)
            cross += jnp.sum(weight * (t - s), axis=1, keepdims=True)
            picked += jnp.sum(jnp.where(hit, s, 0.0), axis=1, keepdims=True)
        lane = lax.broadcasted_iota(jnp.int32, (ROWS, stats_ref.shape[1]), 1)
        out = jnp.zeros(lane.shape, F32)
        for k, value in enumerate((top_s, top_t, mass_s, mass_t, cross, picked)):
            out = jnp.where(lane == k, value, out)
        stats_ref[block, :] = out

    row_blocks(head_ref.shape[0], body)


def backward_kernel(
    spans, ranks, bases_ref, w_any, lse_ref, position_ref, s_head, s_mid, s_tail,
    target_head, target_mid, target_tail,
    g_head, g_mid, g_tail, dz_ref, w_ref, sems,
):
    copies = fetch(w_any, w_ref, sems, spans)
    tiers = (
        (s_head, target_head, g_head), (s_mid, target_mid, g_mid), (s_tail, target_tail, g_tail)
    )

    def body(block):
        position, lse = position_ref[block, :], lse_ref[block, :]
        lse_s, lse_t = lse[:, 0:1], lse[:, 1:2]
        for k, (s_ref, t_ref, g_ref) in enumerate(tiers):
            s, t = s_ref[block, :], t_ref[block, :].astype(F32)
            hit = hits_of(bases_ref[k], position, s.shape)
            g = 2.0 * jnp.exp(s - lse_s) - jnp.exp(t - lse_t) - jnp.where(hit, 1.0, 0.0)
            g_ref[block, :] = g.astype(BF16)

    row_blocks(s_head.shape[0], body)
    rank_mid, rank_tail = ranks
    quarters = len(spans) - 1
    n_vocab, padded, rows = dz_ref.shape
    per = quarters // 2
    depth = rank_mid // per
    parts = []
    for q, (start, size) in enumerate(spans):
        copies[q].wait()
        grad = g_tail if q == quarters else g_mid
        parts.append(dot(w_ref[:, start : start + size], grad[...], 1, 1))
    zeros = jnp.zeros((padded - rank_mid - rank_tail, rows), F32)
    for k in range(n_vocab):
        first = k // 2 * depth
        pieces = [parts[k % 2 * per + q][first : first + depth] for q in range(per)]
        pieces += [parts[quarters][k * rank_tail : (k + 1) * rank_tail], zeros]
        dz_ref[k] = jnp.concatenate(pieces, axis=0).astype(BF16)


def weight_grads_kernel(spans, z_ref, mid_ref, tail_ref, out_ref):
    for q, (start, size) in enumerate(spans):
        grad = tail_ref if q == len(spans) - 1 else mid_ref
        out_ref[:, start : start + size] = dot(z_ref[q], grad[...], 1, 0).astype(BF16)


def hidden_kernel(spans, depth, w_any, g_ref, proj_ref, dz_ref, out_ref, w_ref, sems):
    copies = fetch(w_any, w_ref, sems, spans, spans[0][0])
    n_out, height, _ = out_ref.shape
    n_dp = w_ref.shape[0] // depth
    per = height // depth
    for half in range(n_out // n_dp):
        parts = []
        for q in range(half * per, (half + 1) * per):
            copies[q].wait()
            start = spans[q][0] - spans[0][0]
            parts.append(dot(w_ref[:, start : start + spans[q][1]], g_ref[...], 1, 1))
        for j in range(n_dp):
            k = j * (n_out // n_dp) + half
            rows = slice(j * depth, (j + 1) * depth)
            head = jnp.concatenate([part[rows] for part in parts], axis=0)
            out_ref[k] = (head + dot(proj_ref[k], dz_ref[...], 1, 0)).astype(BF16)


def spread_vocab(block):
    size = lax.axis_size("vocab")
    return lax.all_to_all(jnp.broadcast_to(block[None], (size,) + block.shape), "vocab", 0, 0)


def per_device(
    hidden,
    head_weight,
    proj_mid,
    proj_tail,
    mid_weight,
    tail_weight,
    target_head,
    target_mid,
    target_tail,
    top_ids,
    tier_of,
):
    n_vocab = lax.axis_size("vocab")
    n_dp = lax.axis_size("dp")
    v = lax.axis_index("vocab")
    rows, width = hidden.shape
    depth = head_weight.shape[0]
    rank_mid, rank_tail = proj_mid.shape[1], proj_tail.shape[1]
    ranks = rank_mid + rank_tail

    depth_tail = tail_weight.shape[0]
    quarters, groups = mid_weight.shape[0] // depth_tail, depth // depth_tail
    widths = (head_weight.shape[1], mid_weight.shape[1], tail_weight.shape[1])
    spans = column_spans((quarters, 1, groups), (widths[1], widths[2], widths[0]))
    low, head_spans = spans[: quarters + 1], spans[quarters + 1 :]
    packed_width = spans[-1][0] + spans[-1][1]
    low_width = head_spans[0][0]
    height = n_dp * depth_tail
    vmem, smem, anywhere = (
        pl.BlockSpec(memory_space=space) for space in (pltpu.VMEM, pltpu.SMEM, pl.ANY)
    )

    def shaped(*shape, dtype=BF16):
        return jax.ShapeDtypeStruct(shape, dtype)

    with jax.named_scope("gather_weights"):
        packed = in_vmem(
            functools.partial(pack_kernel, spans, quarters),
            shaped(depth_tail, packed_width),
            mid_weight,
            tail_weight,
            head_weight,
        )
        weights = lax.all_gather(packed, "dp", axis=0, tiled=True)
    with jax.named_scope("gather_proj"):
        packed, proj_mid, proj_tail = lax.optimization_barrier((packed, proj_mid, proj_tail))
        pad = -ranks % 16
        proj_t = jnp.concatenate(
            [proj_mid.T, proj_tail.T, jnp.zeros((pad, depth), BF16)], axis=0
        )
        proj_full = gather_dp(proj_t, 1)
    with jax.named_scope("codes"):
        codes = dot(proj_full, hidden, 1, 1).astype(BF16)
    with jax.named_scope("spread_codes"):
        codes_all = spread_vocab(codes)
    with jax.named_scope("spread_hidden"):
        piece = rows // n_vocab
        mine = lax.dynamic_slice_in_dim(hidden, v * piece, piece, 0)
        mine = mine.reshape(piece, n_dp, depth).transpose(1, 0, 2)
        mine = lax.all_to_all(mine, "dp", 0, 0)
        mine, weights = lax.optimization_barrier((mine, weights))
        x_all = lax.all_gather(mine.reshape(n_dp * piece, depth), "vocab", axis=0)
        x_all = x_all.reshape(n_vocab, n_dp, piece, depth).transpose(1, 0, 2, 3)
        x_all = x_all.reshape(n_dp * rows, depth)
    with jax.named_scope("arrange"):
        hidden_t = hidden.T.reshape(n_dp, groups, depth_tail, rows).transpose(1, 0, 2, 3)
        hidden_t = hidden_t.reshape(groups, height, rows)
        proj_rows = proj_full.T.reshape(n_vocab, width // n_vocab, ranks + pad)
        starts = (0, widths[0] * n_vocab, (widths[0] + widths[1]) * n_vocab)
        bases = jnp.stack([start + v * w for start, w in zip(starts, widths)]).astype(jnp.int32)
        positions = jnp.take(tier_of, top_ids).astype(jnp.int32)[:, None]
        codes_all, hidden_t, proj_rows, positions = lax.optimization_barrier(
            (codes_all, hidden_t, proj_rows, positions)
        )

    with jax.named_scope("logits"):
        z, s_head, s_mid, s_tail, stats = in_vmem(
            functools.partial(forward_kernel, spans, quarters, (rank_mid, rank_tail)),
            (
                shaped(quarters + 1, height, rows),
                shaped(rows, widths[0], dtype=F32),
                shaped(rows, widths[1], dtype=F32),
                shaped(rows, widths[2], dtype=F32),
                shaped(rows, 128, dtype=F32),
            ),
            bases,
            weights,
            codes_all,
            hidden_t,
            positions,
            target_head,
            target_mid,
            target_tail,
            in_specs=[smem, anywhere] + [vmem] * 6,
            scratch_shapes=[
                pltpu.VMEM((height, packed_width), BF16),
                pltpu.SemaphoreType.DMA((len(spans),)),
            ],
        )
    with jax.named_scope("spread_statistics"):
        stats = spread_vocab(stats[:, :8].T)
        near_s, near_t, mass_s, mass_t, cross, picked = (stats[:, k] for k in range(6))
        top_s, top_t = jnp.max(near_s, axis=0), jnp.max(near_t, axis=0)
        scale_s, scale_t = jnp.exp(near_s - top_s[None]), jnp.exp(near_t - top_t[None])
        mass_s = jnp.sum(mass_s * scale_s, axis=0)
        mass_t = jnp.sum(mass_t * scale_t, axis=0)
        cross = jnp.sum(cross * scale_t, axis=0)
        picked = jnp.sum(picked, axis=0)
        lse_s = top_s + jnp.log(mass_s)
        lse_t = top_t + jnp.log(mass_t)
        row_loss = cross / mass_t - lse_t + 2.0 * lse_s - picked
        lse = jnp.stack([lse_s, lse_t], axis=1)
    with jax.named_scope("grad_logits"):
        g_head, g_mid, g_tail, dz = in_vmem(
            functools.partial(backward_kernel, low, (rank_mid, rank_tail)),
            (
                shaped(rows, widths[0]),
                shaped(rows, widths[1]),
                shaped(rows, widths[2]),
                shaped(n_vocab, ranks + pad, rows),
            ),
            bases,
            weights,
            lse,
            positions,
            s_head,
            s_mid,
            s_tail,
            target_head,
            target_mid,
            target_tail,
            in_specs=[smem, anywhere] + [vmem] * 8,
            scratch_shapes=[
                pltpu.VMEM((height, low_width), BF16),
                pltpu.SemaphoreType.DMA((len(low),)),
            ],
        )
    with jax.named_scope("code_grads"):
        dz = lax.all_to_all(dz, "vocab", 0, 0)
        dz = jnp.sum(dz.astype(F32), axis=0).astype(BF16)
    with jax.named_scope("mid_tail_grads"):
        packed_grad = in_vmem(
            functools.partial(weight_grads_kernel, low),
            shaped(height, low_width),
            z,
            g_mid,
            g_tail,
        )
        packed_grad = lax.psum_scatter(packed_grad, "dp", scatter_dimension=0, tiled=True)
        mid_grad, tail_grad = in_vmem(
            functools.partial(unpack_kernel, low),
            (shaped(*mid_weight.shape), shaped(*tail_weight.shape)),
            packed_grad,
        )
    with jax.named_scope("hidden_grad"):
        term = in_vmem(
            functools.partial(hidden_kernel, head_spans, depth_tail),
            shaped(n_vocab, width // n_vocab, rows),
            weights,
            g_head,
            proj_rows,
            dz,
            in_specs=[anywhere] + [vmem] * 3,
            scratch_shapes=[
                pltpu.VMEM((height, packed_width - low_width), BF16),
                pltpu.SemaphoreType.DMA((len(head_spans),)),
            ],
        )
        term = lax.all_to_all(term, "vocab", 0, 0)
    with jax.named_scope("head_proj_grads"):
        g_all = gather_dp(g_head, 0)
        head_grad = dot(x_all, g_all, 0, 0).astype(BF16)
        dz_all = gather_dp(dz, 1)
        proj_grad = dot(x_all, dz_all, 0, 1).astype(BF16)
    with jax.named_scope("hidden_grad_sum"):
        term, head_grad, proj_grad, mid_grad, tail_grad = lax.optimization_barrier(
            (term, head_grad, proj_grad, mid_grad, tail_grad)
        )
        hidden_grad = jnp.sum(term.astype(F32), axis=0).astype(BF16).T
    return (
        head_grad,
        proj_grad[:, :rank_mid],
        proj_grad[:, rank_mid:ranks],
        mid_grad,
        tail_grad,
        hidden_grad,
        row_loss,
    )


def solution(mesh):
    split = P("dp", "vocab")
    in_specs = (P("dp", None),) + (split,) * 8 + (P("dp"), P())
    out_specs = (split,) * 6 + (P("dp"),)
    return jax.shard_map(
        per_device, mesh=mesh, in_specs=in_specs, out_specs=out_specs, check_vma=False
    )
```

```python
import functools

import jax
import jax.numpy as jnp
from jax import lax
from jax.experimental import pallas as pl
from jax.experimental.pallas import tpu as pltpu
from jax.sharding import PartitionSpec as P

BF16 = jnp.bfloat16
F32 = jnp.float32


def dot(left, right, left_dim, right_dim):
    return lax.dot_general(
        left, right, (((left_dim,), (right_dim,)), ((), ())), preferred_element_type=F32
    )


def swap(block, axis_name, flip):
    pairs = [(i, i ^ flip) for i in range(lax.axis_size(axis_name))]
    return lax.ppermute(block, axis_name, pairs)


def ring_near(block, axis_name, step):
    return swap(block, axis_name, step), swap(block, axis_name, 3 * step)


def ring_far(near, other, axis_name, step, half):
    return jnp.concatenate(
        [swap(other[:half], axis_name, step), swap(near[half:], axis_name, 3 * step)], axis=0
    )


def place_kernel(axis, spots_ref, *refs):
    blocks, out, sems = refs[:-2], refs[-2], refs[-1]
    copies = []
    for k, block in enumerate(blocks):
        size = block.shape[axis]
        start = pl.multiple_of(spots_ref[k] * size, size)
        spot = out.at[(slice(None),) * axis + (pl.ds(start, size),)]
        copies.append(pltpu.make_async_copy(block, spot, sems.at[k]))
    for copy in copies:
        copy.start()
    for copy in copies:
        copy.wait()


def place(blocks, spots, axis):
    shape = list(blocks[0].shape)
    shape[axis] *= len(blocks)
    moved = 2 * len(blocks) * blocks[0].size * blocks[0].dtype.itemsize
    return pl.pallas_call(
        functools.partial(place_kernel, axis),
        out_shape=jax.ShapeDtypeStruct(tuple(shape), blocks[0].dtype),
        in_specs=[pl.BlockSpec(memory_space=pltpu.SMEM)]
        + [pl.BlockSpec(memory_space=pltpu.VMEM)] * len(blocks),
        out_specs=pl.BlockSpec(memory_space=pl.ANY),
        scratch_shapes=[pltpu.SemaphoreType.DMA((len(blocks),))],
        compiler_params=pltpu.CompilerParams(vmem_limit_bytes=16 << 20),
        cost_estimate=pl.CostEstimate(flops=0, bytes_accessed=moved, transcendentals=0),
    )(jnp.stack(spots).astype(jnp.int32), *blocks)


def both_cores(parts, axis):
    blocks = [p for part in parts for p in (part, swap(part, "dp", 1))]
    me = lax.axis_index("dp")
    return place(blocks, [me ^ flip for flip in range(len(blocks))], axis)


def gather_dp(block, axis, half):
    near, other = ring_near(block, "dp", 2)
    far = ring_far(near, other, "dp", 2, half)
    return both_cores([block, near, far, other], axis)


def in_vmem(kernel, out_shape, *operands, in_specs=None, scratch_shapes=(), flops=2 * 10**9):
    outs = out_shape if isinstance(out_shape, tuple) else (out_shape,)
    size = sum(a.size * a.dtype.itemsize for a in operands + outs)
    specs = in_specs or [pl.BlockSpec(memory_space=pltpu.VMEM)] * len(operands)
    return pl.pallas_call(
        kernel,
        out_shape=out_shape,
        in_specs=specs,
        scratch_shapes=scratch_shapes,
        compiler_params=pltpu.CompilerParams(vmem_limit_bytes=48 << 20),
        cost_estimate=pl.CostEstimate(flops=flops, bytes_accessed=size, transcendentals=0),
    )(*operands)


def fetch(source, held, sems, spans, base=0):
    copies = [
        pltpu.make_async_copy(
            source.at[:, pl.ds(start, size)], held.at[:, pl.ds(start - base, size)], sems.at[k]
        )
        for k, (start, size) in enumerate(spans)
    ]
    for copy in copies:
        copy.start()
    return copies


def column_spans(groups, widths):
    spans, start = [], 0
    for count, width in zip(groups, widths):
        for _ in range(count):
            spans.append((start, width))
            start += width
    return spans


def pack_kernel(spans, quarters, mid_ref, tail_ref, head_ref, out_ref):
    depth = tail_ref.shape[0]
    mid, head = mid_ref[...].astype(F32), head_ref[...].astype(F32)
    for k, (start, size) in enumerate(spans):
        if k < quarters:
            piece = mid[k * depth : (k + 1) * depth].astype(BF16)
        elif k == quarters:
            piece = tail_ref[...]
        else:
            row = (k - quarters - 1) * depth
            piece = head[row : row + depth].astype(BF16)
        out_ref[:, start : start + size] = piece


def unpack_kernel(spans, packed_ref, mid_ref, tail_ref):
    quarters = [packed_ref[:, a : a + size].astype(F32) for a, size in spans[:-1]]
    mid_ref[...] = jnp.concatenate(quarters, axis=0).astype(BF16)
    start, size = spans[-1]
    tail_ref[...] = packed_ref[:, start : start + size]


ROWS = 16


def row_blocks(rows, body):
    def step(k, carry):
        body(pl.ds(pl.multiple_of(k * ROWS, ROWS), ROWS))
        return carry

    lax.fori_loop(0, rows // ROWS, step, 0)


def hits_of(base, position, shape):
    return position - base == lax.broadcasted_iota(jnp.int32, shape, 1)


def forward_kernel(
    spans, quarters, ranks, bases_ref, w_any, codes_ref, hidden_ref, position_ref,
    target_head, target_mid, target_tail,
    z_ref, head_ref, mid_ref, tail_ref, stats_ref, w_ref, sems,
):
    copies = fetch(w_any, w_ref, sems, spans)
    rank_mid, rank_tail = ranks
    n_dp, per = 2 * codes_ref.shape[0] // quarters, quarters // 2
    depth = rank_mid // per
    codes = [codes_ref[k].astype(F32) for k in range(codes_ref.shape[0])]
    for q in range(quarters):
        first = q % per * depth
        z_ref[q] = jnp.concatenate(
            [codes[2 * j + q // per][first : first + depth] for j in range(n_dp)], axis=0
        ).astype(BF16)
    z_ref[quarters] = jnp.concatenate(
        [code[rank_mid : rank_mid + rank_tail] for code in codes], axis=0
    ).astype(BF16)
    for k, (start, size) in enumerate(spans):
        copies[k].wait()
        weight = w_ref[:, start : start + size]
        if k < quarters:
            part = dot(z_ref[k], weight, 0, 0)
            mid_ref[...] = part if k == 0 else mid_ref[...] + part
        elif k == quarters:
            tail_ref[...] = dot(z_ref[k], weight, 0, 0)
        else:
            part = dot(hidden_ref[k - quarters - 1], weight, 0, 0)
            head_ref[...] = part if k == quarters + 1 else head_ref[...] + part

    tiers = ((head_ref, target_head), (mid_ref, target_mid), (tail_ref, target_tail))

    def body(block):
        pairs = [(s[block, :], t[block, :].astype(F32)) for s, t in tiers]
        position = position_ref[block, :]
        top_s = top_t = None
        for s, t in pairs:
            here_s, here_t = (jnp.max(a, axis=1, keepdims=True) for a in (s, t))
            top_s = here_s if top_s is None else jnp.maximum(top_s, here_s)
            top_t = here_t if top_t is None else jnp.maximum(top_t, here_t)
        mass_s = mass_t = cross = picked = jnp.zeros_like(top_s)
        for k, (s, t) in enumerate(pairs):
            hit = hits_of(bases_ref[k], position, s.shape)
            weight = jnp.exp(t - top_t)
            mass_s += jnp.sum(jnp.exp(s - top_s), axis=1, keepdims=True)
            mass_t += jnp.sum(weight, axis=1, keepdims=True)
            cross += jnp.sum(weight * (t - s), axis=1, keepdims=True)
            picked += jnp.sum(jnp.where(hit, s, 0.0), axis=1, keepdims=True)
        lane = lax.broadcasted_iota(jnp.int32, (ROWS, stats_ref.shape[1]), 1)
        out = jnp.zeros(lane.shape, F32)
        for k, value in enumerate((top_s, top_t, mass_s, mass_t, cross, picked)):
            out = jnp.where(lane == k, value, out)
        stats_ref[block, :] = out

    row_blocks(head_ref.shape[0], body)


def backward_kernel(
    spans, ranks, bases_ref, w_any, lse_ref, position_ref, s_head, s_mid, s_tail,
    target_head, target_mid, target_tail,
    g_head, g_mid, g_tail, dz_ref, w_ref, sems,
):
    copies = fetch(w_any, w_ref, sems, spans)
    tiers = (
        (s_head, target_head, g_head), (s_mid, target_mid, g_mid), (s_tail, target_tail, g_tail)
    )

    def body(block):
        position, lse = position_ref[block, :], lse_ref[block, :]
        lse_s, lse_t = lse[:, 0:1], lse[:, 1:2]
        for k, (s_ref, t_ref, g_ref) in enumerate(tiers):
            s, t = s_ref[block, :], t_ref[block, :].astype(F32)
            hit = hits_of(bases_ref[k], position, s.shape)
            g = 2.0 * jnp.exp(s - lse_s) - jnp.exp(t - lse_t) - jnp.where(hit, 1.0, 0.0)
            g_ref[block, :] = g.astype(BF16)

    row_blocks(s_head.shape[0], body)
    rank_mid, rank_tail = ranks
    quarters = len(spans) - 1
    n_vocab, padded, rows = dz_ref.shape
    per = quarters // 2
    depth = rank_mid // per
    parts = []
    for q, (start, size) in enumerate(spans):
        copies[q].wait()
        grad = g_tail if q == quarters else g_mid
        parts.append(dot(w_ref[:, start : start + size], grad[...], 1, 1))
    zeros = jnp.zeros((padded - rank_mid - rank_tail, rows), F32)
    for k in range(n_vocab):
        first = k // 2 * depth
        pieces = [parts[k % 2 * per + q][first : first + depth] for q in range(per)]
        pieces += [parts[quarters][k * rank_tail : (k + 1) * rank_tail], zeros]
        dz_ref[k] = jnp.concatenate(pieces, axis=0).astype(BF16)


def weight_grads_kernel(spans, z_ref, mid_ref, tail_ref, out_ref):
    for q, (start, size) in enumerate(spans):
        grad = tail_ref if q == len(spans) - 1 else mid_ref
        out_ref[:, start : start + size] = dot(z_ref[q], grad[...], 1, 0).astype(BF16)


def hidden_kernel(
    spans, depth, me_ref, w_any, g_ref, proj_ref, dz_ref,
    a_own, a_near, a_lo, a_hi, a_other, b_own, b_near, b_lo, b_hi, b_other, out_ref, w_ref, sems,
):
    copies = fetch(w_any, w_ref, sems, spans, spans[0][0])
    n_out, height, _ = out_ref.shape
    n_dp = w_ref.shape[0] // depth
    per = height // depth
    for half in range(n_out // n_dp):
        parts = []
        for q in range(half * per, (half + 1) * per):
            copies[q].wait()
            start = spans[q][0] - spans[0][0]
            parts.append(dot(w_ref[:, start : start + spans[q][1]], g_ref[...], 1, 1))
        for j in range(n_dp):
            k = j * (n_out // n_dp) + half
            rows = slice(j * depth, (j + 1) * depth)
            head = jnp.concatenate([part[rows] for part in parts], axis=0)
            out_ref[me_ref[0] ^ k] = (head + dot(proj_ref[k], dz_ref[...], 1, 0)).astype(BF16)
    cut = height // 2
    for k in range(4):
        a_own[k], a_near[k], a_other[k] = (out_ref[4 * z + k, :cut] for z in (0, 1, 3))
        b_own[k], b_near[k], b_other[k] = (out_ref[4 * k + y, cut:] for y in (0, 1, 3))
    for k in range(2):
        a_lo[k], a_hi[k] = out_ref[8 + k, :cut], out_ref[10 + k, :cut]
        b_lo[k], b_hi[k] = out_ref[4 * k + 2, cut:], out_ref[4 * k + 10, cut:]


def fold_kernel(*refs):
    n = len(refs) // 6
    for k in range(n):
        near, hi, other, lo = refs[4 * k : 4 * k + 4]
        near_out, other_out = refs[4 * n + 2 * k : 4 * n + 2 * k + 2]
        cut = lo.shape[0]
        near_out[:cut] = near[:cut]
        near_out[cut:] = (near[cut:].astype(F32) + hi[...].astype(F32)).astype(BF16)
        other_out[:cut] = (other[:cut].astype(F32) + lo[...].astype(F32)).astype(BF16)
        other_out[cut:] = other[cut:]


def total_of(refs):
    return sum(ref[...].astype(F32) for ref in refs)


def turn_kernel(*refs):
    for k in range(2):
        total = total_of(refs[3 * k : 3 * k + 3]).astype(BF16)
        for flip in range(4):
            refs[6 + 4 * k + flip][...] = total[flip]


def end_kernel(*refs):
    total = jnp.concatenate([total_of(refs[:4]), total_of(refs[4:8])], axis=0)
    refs[8][...] = total.T.astype(BF16)


def fold(*rings, beside):
    operands = []
    for near, lo, hi, other, step in rings:
        lo, hi = swap(lo, "vocab", step), swap(hi, "vocab", 3 * step)
        operands += [near, hi, other, lo]
    operands[1], beside = lax.optimization_barrier((operands[1], beside))
    out = in_vmem(
        fold_kernel,
        tuple(
            jax.ShapeDtypeStruct(ring[k].shape, BF16) for ring in rings for k in (0, 3)
        ),
        *operands,
    )
    return [
        (swap(out[2 * k], "vocab", ring[4]), swap(out[2 * k + 1], "vocab", 3 * ring[4]))
        for k, ring in enumerate(rings)
    ] + [beside]


def ring_sums(a, b, early, late):
    (a_near, a_other), (b_near, b_other), early = fold((*a[1:], 4), (*b[1:], 1), beside=early)
    chunk = a[0].shape[1:]
    out = in_vmem(
        turn_kernel,
        (jax.ShapeDtypeStruct(chunk, BF16),) * 8,
        a[0], a_near, a_other, b[0], b_near, b_other,
    )
    moved = [
        part if flip == 0 else swap(part, "vocab", flip * step)
        for step, parts in ((1, out[:4]), (4, out[4:]))
        for flip, part in enumerate(parts)
    ]
    moved[0], late = lax.optimization_barrier((moved[0], late))
    total = in_vmem(
        end_kernel, jax.ShapeDtypeStruct((chunk[1], 2 * chunk[0]), BF16), *moved
    )
    return total, early, late


def spread_vocab(block):
    size = lax.axis_size("vocab")
    return lax.all_to_all(jnp.broadcast_to(block[None], (size,) + block.shape), "vocab", 0, 0)


def per_device(
    hidden,
    head_weight,
    proj_mid,
    proj_tail,
    mid_weight,
    tail_weight,
    target_head,
    target_mid,
    target_tail,
    top_ids,
    tier_of,
):
    n_vocab = lax.axis_size("vocab")
    n_dp = lax.axis_size("dp")
    v = lax.axis_index("vocab")
    rows, width = hidden.shape
    depth = head_weight.shape[0]
    rank_mid, rank_tail = proj_mid.shape[1], proj_tail.shape[1]
    ranks = rank_mid + rank_tail

    depth_tail = tail_weight.shape[0]
    quarters, groups = mid_weight.shape[0] // depth_tail, depth // depth_tail
    widths = (head_weight.shape[1], mid_weight.shape[1], tail_weight.shape[1])
    spans = column_spans((quarters, 1, groups), (widths[1], widths[2], widths[0]))
    low, head_spans = spans[: quarters + 1], spans[quarters + 1 :]
    packed_width = spans[-1][0] + spans[-1][1]
    low_width = head_spans[0][0]
    height = n_dp * depth_tail
    vmem, smem, anywhere = (
        pl.BlockSpec(memory_space=space) for space in (pltpu.VMEM, pltpu.SMEM, pl.ANY)
    )

    def shaped(*shape, dtype=BF16):
        return jax.ShapeDtypeStruct(shape, dtype)

    with jax.named_scope("gather_weights"):
        packed = in_vmem(
            functools.partial(pack_kernel, spans, quarters),
            shaped(depth_tail, packed_width),
            mid_weight,
            tail_weight,
            head_weight,
        )
        weights = lax.all_gather(packed, "dp", axis=0, tiled=True)
    with jax.named_scope("gather_proj"):
        packed, proj_mid, proj_tail = lax.optimization_barrier((packed, proj_mid, proj_tail))
        pad = -ranks % 16
        proj_t = jnp.concatenate(
            [proj_mid.T, proj_tail.T, jnp.zeros((pad, depth), BF16)], axis=0
        )
        proj_full = gather_dp(proj_t, 1, (ranks + pad) // 32 * 16)
    with jax.named_scope("codes"):
        codes = dot(proj_full, hidden, 1, 1).astype(BF16)
    with jax.named_scope("spread_codes"):
        codes_all = spread_vocab(codes)
    with jax.named_scope("spread_hidden"):
        piece = rows // n_vocab
        mine = lax.dynamic_slice_in_dim(hidden, v * piece, piece, 0)
        mine = mine.reshape(piece, n_dp, depth).transpose(1, 0, 2)
        mine = lax.all_to_all(mine, "dp", 0, 0)
        mine, codes_all = lax.optimization_barrier((mine, codes_all))
        x_all = lax.all_gather(mine.reshape(n_dp * piece, depth), "vocab", axis=0)
    with jax.named_scope("arrange"):
        hidden_t = hidden.T.reshape(n_dp, groups, depth_tail, rows).transpose(1, 0, 2, 3)
        hidden_t = hidden_t.reshape(groups, height, rows)
        proj_rows = proj_full.T.reshape(n_vocab, width // n_vocab, ranks + pad)
        starts = (0, widths[0] * n_vocab, (widths[0] + widths[1]) * n_vocab)
        bases = jnp.stack([start + v * w for start, w in zip(starts, widths)]).astype(jnp.int32)
        positions = jnp.take(tier_of, top_ids).astype(jnp.int32)[:, None]
        codes_all, hidden_t, proj_rows, positions = lax.optimization_barrier(
            (codes_all, hidden_t, proj_rows, positions)
        )

    with jax.named_scope("logits"):
        z, s_head, s_mid, s_tail, stats = in_vmem(
            functools.partial(forward_kernel, spans, quarters, (rank_mid, rank_tail)),
            (
                shaped(quarters + 1, height, rows),
                shaped(rows, widths[0], dtype=F32),
                shaped(rows, widths[1], dtype=F32),
                shaped(rows, widths[2], dtype=F32),
                shaped(rows, 128, dtype=F32),
            ),
            bases,
            weights,
            codes_all,
            hidden_t,
            positions,
            target_head,
            target_mid,
            target_tail,
            in_specs=[smem, anywhere] + [vmem] * 6,
            scratch_shapes=[
                pltpu.VMEM((height, packed_width), BF16),
                pltpu.SemaphoreType.DMA((len(spans),)),
            ],
        )
    with jax.named_scope("spread_statistics"):
        stats = spread_vocab(stats[:, :8].T)
        near_s, near_t, mass_s, mass_t, cross, picked = (stats[:, k] for k in range(6))
        top_s, top_t = jnp.max(near_s, axis=0), jnp.max(near_t, axis=0)
        scale_s, scale_t = jnp.exp(near_s - top_s[None]), jnp.exp(near_t - top_t[None])
        mass_s = jnp.sum(mass_s * scale_s, axis=0)
        mass_t = jnp.sum(mass_t * scale_t, axis=0)
        cross = jnp.sum(cross * scale_t, axis=0)
        picked = jnp.sum(picked, axis=0)
        lse_s = top_s + jnp.log(mass_s)
        lse_t = top_t + jnp.log(mass_t)
        row_loss = cross / mass_t - lse_t + 2.0 * lse_s - picked
        lse = jnp.stack([lse_s, lse_t], axis=1)
    with jax.named_scope("grad_logits"):
        g_head, g_mid, g_tail, dz = in_vmem(
            functools.partial(backward_kernel, low, (rank_mid, rank_tail)),
            (
                shaped(rows, widths[0]),
                shaped(rows, widths[1]),
                shaped(rows, widths[2]),
                shaped(n_vocab, ranks + pad, rows),
            ),
            bases,
            weights,
            lse,
            positions,
            s_head,
            s_mid,
            s_tail,
            target_head,
            target_mid,
            target_tail,
            in_specs=[smem, anywhere] + [vmem] * 8,
            scratch_shapes=[
                pltpu.VMEM((height, low_width), BF16),
                pltpu.SemaphoreType.DMA((len(low),)),
            ],
        )
        x_all = x_all.reshape(n_dp * rows, depth)
    with jax.named_scope("head_grad"):
        g_all = gather_dp(g_head.reshape(n_vocab, piece, -1), 1, n_vocab // 2)
        g_all = g_all.reshape(n_dp * rows, -1)
    with jax.named_scope("code_grads"):
        dz = lax.all_to_all(dz, "vocab", 0, 0)
        dz = jnp.sum(dz.astype(F32), axis=0).astype(BF16)
        dz, g_all, x_all = lax.optimization_barrier((dz, g_all, x_all))
    with jax.named_scope("mid_tail_grads"):
        packed_grad = in_vmem(
            functools.partial(weight_grads_kernel, low),
            shaped(height, low_width),
            z,
            g_mid,
            g_tail,
        )
        packed_grad = lax.psum_scatter(packed_grad, "dp", scatter_dimension=0, tiled=True)
        mid_grad, tail_grad = in_vmem(
            functools.partial(unpack_kernel, low),
            (shaped(*mid_weight.shape), shaped(*tail_weight.shape)),
            packed_grad,
        )
    with jax.named_scope("hidden_grad"):
        cut = width // n_vocab // 2
        chunks = [shaped(4, cut, rows)] * 2 + [shaped(2, cut, rows)] * 2 + [shaped(4, cut, rows)]
        pieces = in_vmem(
            functools.partial(hidden_kernel, head_spans, depth_tail),
            tuple(chunks * 2),
            v.astype(jnp.int32).reshape(1),
            weights,
            g_head,
            proj_rows,
            dz,
            in_specs=[smem, anywhere] + [vmem] * 3,
            scratch_shapes=[
                pltpu.VMEM((n_vocab, 2 * cut, rows), BF16),
                pltpu.VMEM((height, packed_width - low_width), BF16),
                pltpu.SemaphoreType.DMA((len(head_spans),)),
            ],
        )
    with jax.named_scope("head_proj_grads"):
        head_grad = dot(x_all, g_all, 0, 0).astype(BF16)
        dz_all = jnp.broadcast_to(dz.T[None], (n_dp, rows, ranks + pad))
        dz_all = lax.all_to_all(dz_all, "dp", 0, 0).reshape(n_dp, n_vocab, piece, -1)
        dz_all = dz_all.transpose(1, 0, 2, 3).reshape(n_dp * rows, -1)
        proj_grad = dot(x_all, dz_all, 0, 0).astype(BF16)
    with jax.named_scope("hidden_grad_sum"):
        hidden_grad, head_grad, late = ring_sums(
            pieces[:5], pieces[5:], head_grad, (proj_grad, mid_grad, tail_grad)
        )
        proj_grad, mid_grad, tail_grad = late
    return (
        head_grad,
        proj_grad[:, :rank_mid],
        proj_grad[:, rank_mid:ranks],
        mid_grad,
        tail_grad,
        hidden_grad,
        row_loss,
    )


def solution(mesh):
    split = P("dp", "vocab")
    in_specs = (P("dp", None),) + (split,) * 8 + (P("dp"), P())
    out_specs = (split,) * 6 + (P("dp"),)
    return jax.shard_map(
        per_device, mesh=mesh, in_specs=in_specs, out_specs=out_specs, check_vma=False
    )
```

```python
import functools

import jax
import jax.numpy as jnp
from jax import lax
from jax.experimental import pallas as pl
from jax.experimental.pallas import tpu as pltpu
from jax.sharding import PartitionSpec as P

BF16 = jnp.bfloat16
F32 = jnp.float32


def dot(left, right, left_dim, right_dim):
    return lax.dot_general(
        left, right, (((left_dim,), (right_dim,)), ((), ())), preferred_element_type=F32
    )


def swap(block, axis_name, flip):
    pairs = [(i, i ^ flip) for i in range(lax.axis_size(axis_name))]
    return lax.ppermute(block, axis_name, pairs)


def ring_near(block, axis_name, step):
    return swap(block, axis_name, step), swap(block, axis_name, 3 * step)


def ring_far(near, other, axis_name, step, half):
    return jnp.concatenate(
        [swap(other[:half], axis_name, step), swap(near[half:], axis_name, 3 * step)], axis=0
    )


def place_kernel(axis, spots_ref, *refs):
    blocks, out, sems = refs[:-2], refs[-2], refs[-1]
    copies = []
    for k, block in enumerate(blocks):
        size = block.shape[axis]
        start = pl.multiple_of(spots_ref[k] * size, size)
        spot = out.at[(slice(None),) * axis + (pl.ds(start, size),)]
        copies.append(pltpu.make_async_copy(block, spot, sems.at[k]))
    for copy in copies:
        copy.start()
    for copy in copies:
        copy.wait()


def place(blocks, spots, axis):
    shape = list(blocks[0].shape)
    shape[axis] *= len(blocks)
    moved = 2 * len(blocks) * blocks[0].size * blocks[0].dtype.itemsize
    return pl.pallas_call(
        functools.partial(place_kernel, axis),
        out_shape=jax.ShapeDtypeStruct(tuple(shape), blocks[0].dtype),
        in_specs=[pl.BlockSpec(memory_space=pltpu.SMEM)]
        + [pl.BlockSpec(memory_space=pltpu.VMEM)] * len(blocks),
        out_specs=pl.BlockSpec(memory_space=pl.ANY),
        scratch_shapes=[pltpu.SemaphoreType.DMA((len(blocks),))],
        compiler_params=pltpu.CompilerParams(vmem_limit_bytes=16 << 20),
        cost_estimate=pl.CostEstimate(flops=0, bytes_accessed=moved, transcendentals=0),
    )(jnp.stack(spots).astype(jnp.int32), *blocks)


def both_cores(parts, axis):
    blocks = [p for part in parts for p in (part, swap(part, "dp", 1))]
    me = lax.axis_index("dp")
    return place(blocks, [me ^ flip for flip in range(len(blocks))], axis)


def gather_dp(block, axis, half):
    near, other = ring_near(block, "dp", 2)
    far = ring_far(near, other, "dp", 2, half)
    return both_cores([block, near, far, other], axis)


def in_vmem(kernel, out_shape, *operands, in_specs=None, out_specs=None, scratch_shapes=(), mib=16):
    outs = out_shape if isinstance(out_shape, tuple) else (out_shape,)
    size = sum(a.size * a.dtype.itemsize for a in operands + outs)
    specs = in_specs or [pl.BlockSpec(memory_space=pltpu.VMEM)] * len(operands)
    return pl.pallas_call(
        kernel,
        out_shape=out_shape,
        in_specs=specs,
        out_specs=out_specs or jax.tree.map(lambda _: pl.BlockSpec(memory_space=pltpu.VMEM), out_shape),
        scratch_shapes=scratch_shapes,
        compiler_params=pltpu.CompilerParams(vmem_limit_bytes=mib << 20),
        cost_estimate=pl.CostEstimate(flops=2 * 10**9, bytes_accessed=size, transcendentals=0),
    )(*operands)


def fetch(source, held, sems, spans, base=0, first=0):
    copies = [
        pltpu.make_async_copy(
            source.at[:, pl.ds(start, size)], held.at[:, pl.ds(start - base, size)], sems.at[first + k]
        )
        for k, (start, size) in enumerate(spans)
    ]
    for copy in copies:
        copy.start()
    return copies


def column_spans(groups, widths):
    spans, start = [], 0
    for count, width in zip(groups, widths):
        for _ in range(count):
            spans.append((start, width))
            start += width
    return spans


def pack_kernel(spans, quarters, mid_ref, tail_ref, head_ref, out_ref):
    depth = tail_ref.shape[0]
    mid, head = mid_ref[...].astype(F32), head_ref[...].astype(F32)
    for k, (start, size) in enumerate(spans):
        if k < quarters:
            piece = mid[k * depth : (k + 1) * depth].astype(BF16)
        elif k == quarters:
            piece = tail_ref[...]
        else:
            row = (k - quarters - 1) * depth
            piece = head[row : row + depth].astype(BF16)
        out_ref[:, start : start + size] = piece


def unpack_kernel(spans, packed_ref, mid_ref, tail_ref):
    quarters = [packed_ref[:, a : a + size].astype(F32) for a, size in spans[:-1]]
    mid_ref[...] = jnp.concatenate(quarters, axis=0).astype(BF16)
    start, size = spans[-1]
    tail_ref[...] = packed_ref[:, start : start + size]


ROWS = 32
UNROLL = 2


def row_blocks(rows, body):
    def step(k, carry):
        body(pl.ds(pl.multiple_of(k * ROWS, ROWS), ROWS))
        return carry

    lax.fori_loop(0, rows // ROWS, step, 0, unroll=UNROLL)


def hits_of(base, position, shape):
    return position - base == lax.broadcasted_iota(jnp.int32, shape, 1)


def add_statistics(bases_ref, tiers, position_ref, stats_ref, block, first):
    pairs = [(k, s[block, :], t[block, :].astype(F32)) for k, s, t in tiers]
    position = position_ref[block, :]
    old = stats_ref[block, :]
    column = [old[:, k : k + 1] for k in range(6)]
    top_s, top_t = (None, None) if first else column[:2]
    for _, s, t in pairs:
        here_s, here_t = (jnp.max(a, axis=1, keepdims=True) for a in (s, t))
        top_s = here_s if top_s is None else jnp.maximum(top_s, here_s)
        top_t = here_t if top_t is None else jnp.maximum(top_t, here_t)
    if first:
        mass_s = mass_t = cross = picked = jnp.zeros_like(top_s)
    else:
        scale_s, scale_t = jnp.exp(column[0] - top_s), jnp.exp(column[1] - top_t)
        mass_s, mass_t, cross = column[2] * scale_s, column[3] * scale_t, column[4] * scale_t
        picked = column[5]
    for k, s, t in pairs:
        hit = hits_of(bases_ref[k], position, s.shape)
        weight = jnp.exp(t - top_t)
        mass_s += jnp.sum(jnp.exp(s - top_s), axis=1, keepdims=True)
        mass_t += jnp.sum(weight, axis=1, keepdims=True)
        cross += jnp.sum(weight * (t - s), axis=1, keepdims=True)
        picked += jnp.sum(jnp.where(hit, s, 0.0), axis=1, keepdims=True)
    lane = lax.broadcasted_iota(jnp.int32, (ROWS, stats_ref.shape[1]), 1)
    out = jnp.zeros(lane.shape, F32)
    for k, value in enumerate((top_s, top_t, mass_s, mass_t, cross, picked)):
        out = jnp.where(lane == k, value, out)
    stats_ref[block, :] = out


def forward_kernel(
    spans, quarters, ranks, bases_ref, w_any, codes_ref, hidden_any, position_ref,
    target_head, target_mid, target_tail,
    z_ref, head_any, mid_any, tail_any, stats_ref,
    w_ref, hidden_ref, head_ref, mid_ref, tail_ref, sems, out_sems,
):
    low = quarters + 1
    copies = fetch(w_any, w_ref, sems, spans[:low])
    hidden_copy = pltpu.make_async_copy(hidden_any, hidden_ref, out_sems.at[3])
    hidden_copy.start()
    copies += fetch(w_any, w_ref, sems, spans[low:], first=low)
    rank_mid, rank_tail = ranks
    n_dp, per = 2 * codes_ref.shape[0] // quarters, quarters // 2
    depth = rank_mid // per
    codes = [codes_ref[k].astype(F32) for k in range(codes_ref.shape[0])]
    for q in range(quarters):
        first = q % per * depth
        z_ref[q] = jnp.concatenate(
            [codes[2 * j + q // per][first : first + depth] for j in range(n_dp)], axis=0
        ).astype(BF16)
    z_ref[quarters] = jnp.concatenate(
        [code[rank_mid : rank_mid + rank_tail] for code in codes], axis=0
    ).astype(BF16)

    def weight(k):
        copies[k].wait()
        return w_ref[:, spans[k][0] : spans[k][0] + spans[k][1]]

    outs = [
        pltpu.make_async_copy(ref, out, out_sems.at[k])
        for k, (ref, out) in enumerate(
            ((mid_ref, mid_any), (tail_ref, tail_any), (head_ref, head_any))
        )
    ]
    for q in range(quarters):
        part = dot(z_ref[q], weight(q), 0, 0)
        mid_ref[...] = part if q == 0 else mid_ref[...] + part
    outs[0].start()
    tail_ref[...] = dot(z_ref[quarters], weight(quarters), 0, 0)
    outs[1].start()
    rows = head_ref.shape[0]
    tiers = ((1, mid_ref, target_mid), (2, tail_ref, target_tail))
    row_blocks(
        rows,
        lambda block: add_statistics(bases_ref, tiers, position_ref, stats_ref, block, True),
    )
    hidden_copy.wait()
    for k in range(low, len(spans)):
        part = dot(hidden_ref[k - low], weight(k), 0, 0)
        head_ref[...] = part if k == low else head_ref[...] + part
    outs[2].start()
    tiers_head = ((0, head_ref, target_head),)
    row_blocks(
        rows,
        lambda block: add_statistics(bases_ref, tiers_head, position_ref, stats_ref, block, False),
    )
    for copy in outs:
        copy.wait()


def backward_kernel(
    spans, ranks, bases_ref, w_any, lse_ref, position_ref, s_head, s_mid, s_tail,
    target_head, target_mid, target_tail,
    g_head, g_mid, g_tail, dz_ref, w_ref, sems,
):
    copies = fetch(w_any, w_ref, sems, spans)
    tiers = (
        (s_head, target_head, g_head), (s_mid, target_mid, g_mid), (s_tail, target_tail, g_tail)
    )

    def body(block):
        position, lse = position_ref[block, :], lse_ref[block, :]
        lse_s, lse_t = lse[:, 0:1], lse[:, 1:2]
        for k, (s_ref, t_ref, g_ref) in enumerate(tiers):
            s, t = s_ref[block, :], t_ref[block, :].astype(F32)
            hit = hits_of(bases_ref[k], position, s.shape)
            g = 2.0 * jnp.exp(s - lse_s) - jnp.exp(t - lse_t) - jnp.where(hit, 1.0, 0.0)
            g_ref[block, :] = g.astype(BF16)

    row_blocks(s_head.shape[0], body)
    rank_mid, rank_tail = ranks
    quarters = len(spans) - 1
    n_vocab, padded, rows = dz_ref.shape
    per = quarters // 2
    depth = rank_mid // per
    parts = []
    for q, (start, size) in enumerate(spans):
        copies[q].wait()
        grad = g_tail if q == quarters else g_mid
        parts.append(dot(w_ref[:, start : start + size], grad[...], 1, 1))
    zeros = jnp.zeros((padded - rank_mid - rank_tail, rows), F32)
    for k in range(n_vocab):
        first = k // 2 * depth
        pieces = [parts[k % 2 * per + q][first : first + depth] for q in range(per)]
        pieces += [parts[quarters][k * rank_tail : (k + 1) * rank_tail], zeros]
        dz_ref[k] = jnp.concatenate(pieces, axis=0).astype(BF16)


def weight_grads_kernel(spans, z_ref, mid_ref, tail_ref, out_any, out_ref, sems):
    copies = []
    for q, (start, size) in enumerate(spans):
        grad = tail_ref if q == len(spans) - 1 else mid_ref
        columns = pl.ds(start, size)
        out_ref[:, columns] = dot(z_ref[q], grad[...], 1, 0).astype(BF16)
        copies.append(
            pltpu.make_async_copy(out_ref.at[:, columns], out_any.at[:, columns], sems.at[q])
        )
        copies[-1].start()
    for copy in copies:
        copy.wait()


def hidden_head_kernel(spans, depth, me_ref, w_any, g_ref, out_ref, w_ref, sems):
    copies = fetch(w_any, w_ref, sems, spans, spans[0][0])
    n_out, height, _ = out_ref.shape
    n_dp = w_ref.shape[0] // depth
    per = height // depth
    for half in range(n_out // n_dp):
        parts = []
        for q in range(half * per, (half + 1) * per):
            copies[q].wait()
            start = spans[q][0] - spans[0][0]
            parts.append(dot(w_ref[:, start : start + spans[q][1]], g_ref[...], 1, 1))
        for j in range(n_dp):
            k = j * (n_out // n_dp) + half
            rows = slice(j * depth, (j + 1) * depth)
            head = jnp.concatenate([part[rows] for part in parts], axis=0)
            out_ref[me_ref[0] ^ k] = head.astype(BF16)


def hidden_kernel(
    me_ref, head_ref, proj_ref, dz_ref,
    a_own, a_near, a_lo, a_hi, a_other, b_own, b_near, b_lo, b_hi, b_other,
):
    cut = head_ref.shape[1] // 2
    a_refs = (a_own, a_near, (a_lo, a_hi), a_other)
    b_refs = (b_own, b_near, (b_lo, b_hi), b_other)
    for flip in range(head_ref.shape[0]):
        proj = proj_ref[me_ref[0] ^ flip]
        term = (head_ref[flip].astype(F32) + dot(proj, dz_ref[...], 1, 0)).astype(BF16)
        z, y = flip // 4, flip % 4
        for refs, chunk, k, part in ((a_refs, z, y, term[:cut]), (b_refs, y, z, term[cut:])):
            if chunk == 2:
                refs[2][k // 2][k % 2] = part
            else:
                refs[chunk][k] = part


def fold_kernel(*refs):
    n = len(refs) // 6
    for k in range(n):
        near, hi, other, lo = refs[4 * k : 4 * k + 4]
        near_out, other_out = refs[4 * n + 2 * k : 4 * n + 2 * k + 2]
        cut = lo.shape[0]
        near_out[:cut] = near[:cut]
        near_out[cut:] = (near[cut:].astype(F32) + hi[...].astype(F32)).astype(BF16)
        other_out[:cut] = (other[:cut].astype(F32) + lo[...].astype(F32)).astype(BF16)
        other_out[cut:] = other[cut:]


def total_of(refs):
    return sum(ref[...].astype(F32) for ref in refs)


def turn_kernel(*refs):
    for k in range(2):
        total = total_of(refs[3 * k : 3 * k + 3]).astype(BF16)
        for flip in range(4):
            refs[6 + 4 * k + flip][...] = total[flip]


def end_kernel(*refs):
    total = jnp.concatenate([total_of(refs[:4]), total_of(refs[4:8])], axis=0)
    refs[8][...] = total.astype(BF16)


def fold(*rings, beside):
    operands = []
    for near, lo, hi, other, step in rings:
        lo, hi = swap(lo, "vocab", step), swap(hi, "vocab", 3 * step)
        operands += [near, hi, other, lo]
    operands[1], beside = lax.optimization_barrier((operands[1], beside))
    out = in_vmem(
        fold_kernel,
        tuple(
            jax.ShapeDtypeStruct(ring[k].shape, BF16) for ring in rings for k in (0, 3)
        ),
        *operands,
    )
    return [
        (swap(out[2 * k], "vocab", ring[4]), swap(out[2 * k + 1], "vocab", 3 * ring[4]))
        for k, ring in enumerate(rings)
    ] + [beside]


def ring_sums(a, b, early, dz, middle, late):
    (a_near, a_other), (b_near, b_other), (early, dz) = fold(
        (*a[1:], 4), (*b[1:], 1), beside=(early, dz)
    )
    middle = middle(dz)
    chunk = a[0].shape[1:]
    out = in_vmem(
        turn_kernel,
        (jax.ShapeDtypeStruct(chunk, BF16),) * 8,
        a[0], a_near, a_other, b[0], b_near, b_other,
    )
    moved = [
        part if flip == 0 else swap(part, "vocab", flip * step)
        for step, parts in ((1, out[:4]), (4, out[4:]))
        for flip, part in enumerate(parts)
    ]
    moved[0], middle, late = lax.optimization_barrier((moved[0], middle, late))
    total = in_vmem(
        end_kernel, jax.ShapeDtypeStruct((2 * chunk[0], chunk[1]), BF16), *moved
    )
    return total.T, early, middle, late


def spread_vocab(block):
    size = lax.axis_size("vocab")
    return lax.all_to_all(jnp.broadcast_to(block[None], (size,) + block.shape), "vocab", 0, 0)


def per_device(
    hidden,
    head_weight,
    proj_mid,
    proj_tail,
    mid_weight,
    tail_weight,
    target_head,
    target_mid,
    target_tail,
    top_ids,
    tier_of,
):
    n_vocab = lax.axis_size("vocab")
    n_dp = lax.axis_size("dp")
    v = lax.axis_index("vocab")
    rows, width = hidden.shape
    depth = head_weight.shape[0]
    rank_mid, rank_tail = proj_mid.shape[1], proj_tail.shape[1]
    ranks = rank_mid + rank_tail

    depth_tail = tail_weight.shape[0]
    quarters, groups = mid_weight.shape[0] // depth_tail, depth // depth_tail
    widths = (head_weight.shape[1], mid_weight.shape[1], tail_weight.shape[1])
    spans = column_spans((quarters, 1, groups), (widths[1], widths[2], widths[0]))
    low, head_spans = spans[: quarters + 1], spans[quarters + 1 :]
    packed_width = spans[-1][0] + spans[-1][1]
    low_width = head_spans[0][0]
    height = n_dp * depth_tail
    vmem, smem, anywhere = (
        pl.BlockSpec(memory_space=space) for space in (pltpu.VMEM, pltpu.SMEM, pl.ANY)
    )

    def shaped(*shape, dtype=BF16):
        return jax.ShapeDtypeStruct(shape, dtype)

    with jax.named_scope("gather_weights"):
        packed = in_vmem(
            functools.partial(pack_kernel, spans, quarters),
            shaped(depth_tail, packed_width),
            mid_weight,
            tail_weight,
            head_weight,
        )
        weights = lax.all_gather(packed, "dp", axis=0, tiled=True)
    with jax.named_scope("gather_proj"):
        packed, proj_mid, proj_tail = lax.optimization_barrier((packed, proj_mid, proj_tail))
        pad = -ranks % 16
        proj_t = jnp.concatenate(
            [proj_mid.T, proj_tail.T, jnp.zeros((pad, depth), BF16)], axis=0
        )
        proj_full = gather_dp(proj_t, 1, (ranks + pad) // 32 * 16)
    with jax.named_scope("codes"):
        codes = dot(proj_full, hidden, 1, 1).astype(BF16)
    with jax.named_scope("spread_codes"):
        codes_all = spread_vocab(codes)
    with jax.named_scope("spread_hidden"):
        piece = rows // n_vocab
        mine = lax.dynamic_slice_in_dim(hidden, v * piece, piece, 0)
        mine = mine.reshape(piece, n_dp, depth).transpose(1, 0, 2)
        mine = lax.all_to_all(mine, "dp", 0, 0)
        mine, codes_all = lax.optimization_barrier((mine, codes_all))
        x_all = lax.all_gather(mine.reshape(n_dp * piece, depth), "vocab", axis=0)
    with jax.named_scope("arrange"):
        hidden_t = hidden.T.reshape(n_dp, groups, depth_tail, rows).transpose(1, 0, 2, 3)
        hidden_t = hidden_t.reshape(groups, height, rows)
        proj_rows = proj_full.T.reshape(n_vocab, width // n_vocab, ranks + pad)
        starts = (0, widths[0] * n_vocab, (widths[0] + widths[1]) * n_vocab)
        bases = jnp.stack([start + v * w for start, w in zip(starts, widths)]).astype(jnp.int32)
        positions = jnp.take(tier_of, top_ids).astype(jnp.int32)[:, None]
        codes_all, hidden_t, proj_rows, positions = lax.optimization_barrier(
            (codes_all, hidden_t, proj_rows, positions)
        )

    with jax.named_scope("logits"):
        z, s_head, s_mid, s_tail, stats = in_vmem(
            functools.partial(forward_kernel, spans, quarters, (rank_mid, rank_tail)),
            (
                shaped(quarters + 1, height, rows),
                shaped(rows, widths[0], dtype=F32),
                shaped(rows, widths[1], dtype=F32),
                shaped(rows, widths[2], dtype=F32),
                shaped(rows, 128, dtype=F32),
            ),
            bases,
            weights,
            codes_all,
            hidden_t,
            positions,
            target_head,
            target_mid,
            target_tail,
            in_specs=[smem, anywhere, vmem, anywhere] + [vmem] * 4,
            out_specs=(vmem, anywhere, anywhere, anywhere, vmem),
            scratch_shapes=[
                pltpu.VMEM((height, packed_width), BF16),
                pltpu.VMEM(hidden_t.shape, BF16),
                pltpu.VMEM((rows, widths[0]), F32),
                pltpu.VMEM((rows, widths[1]), F32),
                pltpu.VMEM((rows, widths[2]), F32),
                pltpu.SemaphoreType.DMA((len(spans),)),
                pltpu.SemaphoreType.DMA((4,)),
            ],
            mib=48,
        )
    with jax.named_scope("spread_statistics"):
        stats = spread_vocab(stats[:, :8].T)
        near_s, near_t, mass_s, mass_t, cross, picked = (stats[:, k] for k in range(6))
        top_s, top_t = jnp.max(near_s, axis=0), jnp.max(near_t, axis=0)
        scale_s, scale_t = jnp.exp(near_s - top_s[None]), jnp.exp(near_t - top_t[None])
        mass_s = jnp.sum(mass_s * scale_s, axis=0)
        mass_t = jnp.sum(mass_t * scale_t, axis=0)
        cross = jnp.sum(cross * scale_t, axis=0)
        picked = jnp.sum(picked, axis=0)
        lse_s = top_s + jnp.log(mass_s)
        lse_t = top_t + jnp.log(mass_t)
        row_loss = cross / mass_t - lse_t + 2.0 * lse_s - picked
        lse = jnp.stack([lse_s, lse_t], axis=1)
    with jax.named_scope("grad_logits"):
        g_head, g_mid, g_tail, dz = in_vmem(
            functools.partial(backward_kernel, low, (rank_mid, rank_tail)),
            (
                shaped(rows, widths[0]),
                shaped(rows, widths[1]),
                shaped(rows, widths[2]),
                shaped(n_vocab, ranks + pad, rows),
            ),
            bases,
            weights,
            lse,
            positions,
            s_head,
            s_mid,
            s_tail,
            target_head,
            target_mid,
            target_tail,
            in_specs=[smem, anywhere] + [vmem] * 8,
            scratch_shapes=[
                pltpu.VMEM((height, low_width), BF16),
                pltpu.SemaphoreType.DMA((len(low),)),
            ],
            mib=48,
        )
        x_all = x_all.reshape(n_dp * rows, depth)
    with jax.named_scope("hidden_head"):
        me = v.astype(jnp.int32).reshape(1)
        cut = width // n_vocab // 2
        head_term = in_vmem(
            functools.partial(hidden_head_kernel, head_spans, depth_tail),
            shaped(n_vocab, 2 * cut, rows),
            me,
            weights,
            g_head,
            in_specs=[smem, anywhere, vmem],
            scratch_shapes=[
                pltpu.VMEM((height, packed_width - low_width), BF16),
                pltpu.SemaphoreType.DMA((len(head_spans),)),
            ],
            mib=48,
        )
    with jax.named_scope("head_grad"):
        g_rows = g_head.reshape(n_vocab, piece, -1)
        g_near, g_other = ring_near(g_rows, "dp", 2)
        g_near, g_other, head_term = lax.optimization_barrier((g_near, g_other, head_term))
        g_far = ring_far(g_near, g_other, "dp", 2, n_vocab // 2)
        g_all = both_cores([g_rows, g_near, g_far, g_other], 1)
        g_all = g_all.reshape(n_dp * rows, -1)
    with jax.named_scope("code_grads"):
        dz = lax.all_to_all(dz, "vocab", 0, 0)
        dz = jnp.sum(dz.astype(F32), axis=0).astype(BF16)
        dz, g_all, x_all = lax.optimization_barrier((dz, g_all, x_all))
    with jax.named_scope("mid_tail_grads"):
        packed_grad = in_vmem(
            functools.partial(weight_grads_kernel, low),
            shaped(height, low_width),
            z,
            g_mid,
            g_tail,
            out_specs=anywhere,
            scratch_shapes=[
                pltpu.VMEM((height, low_width), BF16),
                pltpu.SemaphoreType.DMA((len(low),)),
            ],
            mib=48,
        )
        packed_grad = lax.psum_scatter(packed_grad, "dp", scatter_dimension=0, tiled=True)
        mid_grad, tail_grad = in_vmem(
            functools.partial(unpack_kernel, low),
            (shaped(*mid_weight.shape), shaped(*tail_weight.shape)),
            packed_grad,
        )
    with jax.named_scope("hidden_grad"):
        chunks = [shaped(4, cut, rows)] * 2 + [shaped(2, cut, rows)] * 2 + [shaped(4, cut, rows)]
        pieces = in_vmem(
            hidden_kernel,
            tuple(chunks * 2),
            me,
            head_term,
            proj_rows,
            dz,
            in_specs=[smem] + [vmem] * 3,
            mib=48,
        )
    with jax.named_scope("head_proj_grads"):
        head_grad = dot(x_all, g_all, 0, 0).astype(BF16)

    def proj_grads(dz):
        with jax.named_scope("head_proj_grads"):
            dz_all = jnp.broadcast_to(dz.T[None], (n_dp, rows, ranks + pad))
            dz_all = lax.all_to_all(dz_all, "dp", 0, 0).reshape(n_dp, n_vocab, piece, -1)
            dz_all = dz_all.transpose(1, 0, 2, 3).reshape(n_dp * rows, -1)
            return dot(dz_all, x_all, 0, 0).astype(BF16)

    with jax.named_scope("hidden_grad_sum"):
        hidden_grad, head_grad, proj_grad, (mid_grad, tail_grad) = ring_sums(
            pieces[:5], pieces[5:], head_grad, dz, proj_grads, (mid_grad, tail_grad)
        )
    return (
        head_grad,
        proj_grad[:rank_mid].T,
        proj_grad[rank_mid:ranks].T,
        mid_grad,
        tail_grad,
        hidden_grad,
        row_loss,
    )


def solution(mesh):
    split = P("dp", "vocab")
    in_specs = (P("dp", None),) + (split,) * 8 + (P("dp"), P())
    out_specs = (split,) * 6 + (P("dp"),)
    return jax.shard_map(
        per_device, mesh=mesh, in_specs=in_specs, out_specs=out_specs, check_vma=False
    )
```

```python
import functools

import jax
import jax.numpy as jnp
from jax import lax
from jax.experimental import pallas as pl
from jax.experimental.pallas import tpu as pltpu
from jax.sharding import PartitionSpec as P

BF16 = jnp.bfloat16
F32 = jnp.float32


def dot(left, right, left_dim, right_dim):
    return lax.dot_general(
        left, right, (((left_dim,), (right_dim,)), ((), ())), preferred_element_type=F32
    )


def swap(block, axis_name, flip):
    pairs = [(i, i ^ flip) for i in range(lax.axis_size(axis_name))]
    return lax.ppermute(block, axis_name, pairs)


def ring_near(block, axis_name, step):
    return swap(block, axis_name, step), swap(block, axis_name, 3 * step)


def ring_far(near, other, axis_name, step, half):
    return jnp.concatenate(
        [swap(other[:half], axis_name, step), swap(near[half:], axis_name, 3 * step)], axis=0
    )


def place_kernel(axis, spots_ref, *refs):
    blocks, out, sems = refs[:-2], refs[-2], refs[-1]
    copies = []
    for k, block in enumerate(blocks):
        size = block.shape[axis]
        start = pl.multiple_of(spots_ref[k] * size, size)
        spot = out.at[(slice(None),) * axis + (pl.ds(start, size),)]
        copies.append(pltpu.make_async_copy(block, spot, sems.at[k]))
    for copy in copies:
        copy.start()
    for copy in copies:
        copy.wait()


def place(blocks, spots, axis):
    shape = list(blocks[0].shape)
    shape[axis] *= len(blocks)
    moved = 2 * len(blocks) * blocks[0].size * blocks[0].dtype.itemsize
    return pl.pallas_call(
        functools.partial(place_kernel, axis),
        out_shape=jax.ShapeDtypeStruct(tuple(shape), blocks[0].dtype),
        in_specs=[pl.BlockSpec(memory_space=pltpu.SMEM)]
        + [pl.BlockSpec(memory_space=pltpu.VMEM)] * len(blocks),
        out_specs=pl.BlockSpec(memory_space=pl.ANY),
        scratch_shapes=[pltpu.SemaphoreType.DMA((len(blocks),))],
        compiler_params=pltpu.CompilerParams(vmem_limit_bytes=16 << 20),
        cost_estimate=pl.CostEstimate(flops=0, bytes_accessed=moved, transcendentals=0),
    )(jnp.stack(spots).astype(jnp.int32), *blocks)


def both_cores(parts, axis):
    blocks = [p for part in parts for p in (part, swap(part, "dp", 1))]
    me = lax.axis_index("dp")
    return place(blocks, [me ^ flip for flip in range(len(blocks))], axis)


def gather_dp(block, axis, half):
    near, other = ring_near(block, "dp", 2)
    far = ring_far(near, other, "dp", 2, half)
    return both_cores([block, near, far, other], axis)


def in_vmem(kernel, out_shape, *operands, in_specs=None, out_specs=None, scratch_shapes=(), mib=16):
    outs = out_shape if isinstance(out_shape, tuple) else (out_shape,)
    size = sum(a.size * a.dtype.itemsize for a in operands + outs)
    specs = in_specs or [pl.BlockSpec(memory_space=pltpu.VMEM)] * len(operands)
    return pl.pallas_call(
        kernel,
        out_shape=out_shape,
        in_specs=specs,
        out_specs=out_specs or jax.tree.map(lambda _: pl.BlockSpec(memory_space=pltpu.VMEM), out_shape),
        scratch_shapes=scratch_shapes,
        compiler_params=pltpu.CompilerParams(vmem_limit_bytes=mib << 20),
        cost_estimate=pl.CostEstimate(flops=2 * 10**9, bytes_accessed=size, transcendentals=0),
    )(*operands)


def fetch(source, held, sems, spans, base=0, first=0):
    copies = [
        pltpu.make_async_copy(
            source.at[:, pl.ds(start, size)], held.at[:, pl.ds(start - base, size)], sems.at[first + k]
        )
        for k, (start, size) in enumerate(spans)
    ]
    for copy in copies:
        copy.start()
    return copies


def column_spans(groups, widths):
    spans, start = [], 0
    for count, width in zip(groups, widths):
        for _ in range(count):
            spans.append((start, width))
            start += width
    return spans


def pack_kernel(spans, quarters, mid_ref, tail_ref, head_ref, out_ref):
    depth = tail_ref.shape[0]
    mid, head = mid_ref[...].astype(F32), head_ref[...].astype(F32)
    for k, (start, size) in enumerate(spans):
        if k < quarters:
            piece = mid[k * depth : (k + 1) * depth].astype(BF16)
        elif k == quarters:
            piece = tail_ref[...]
        else:
            row = (k - quarters - 1) * depth
            piece = head[row : row + depth].astype(BF16)
        out_ref[:, start : start + size] = piece


def unpack_kernel(spans, packed_ref, mid_ref, tail_ref):
    quarters = [packed_ref[:, a : a + size].astype(F32) for a, size in spans[:-1]]
    mid_ref[...] = jnp.concatenate(quarters, axis=0).astype(BF16)
    start, size = spans[-1]
    tail_ref[...] = packed_ref[:, start : start + size]


ROWS = 32
UNROLL = 2


def row_blocks(rows, body):
    def step(k, carry):
        body(pl.ds(pl.multiple_of(k * ROWS, ROWS), ROWS))
        return carry

    lax.fori_loop(0, rows // ROWS, step, 0, unroll=UNROLL)


def hits_of(base, position, shape):
    return position - base == lax.broadcasted_iota(jnp.int32, shape, 1)


def add_statistics(bases_ref, tiers, position_ref, stats_ref, block, first):
    pairs = [(k, s[block, :], t[block, :].astype(F32)) for k, s, t in tiers]
    position = position_ref[block, :]
    old = stats_ref[block, :]
    column = [old[:, k : k + 1] for k in range(6)]
    top_s, top_t = (None, None) if first else column[:2]
    for _, s, t in pairs:
        here_s, here_t = (jnp.max(a, axis=1, keepdims=True) for a in (s, t))
        top_s = here_s if top_s is None else jnp.maximum(top_s, here_s)
        top_t = here_t if top_t is None else jnp.maximum(top_t, here_t)
    if first:
        mass_s = mass_t = cross = picked = jnp.zeros_like(top_s)
    else:
        scale_s, scale_t = jnp.exp(column[0] - top_s), jnp.exp(column[1] - top_t)
        mass_s, mass_t, cross = column[2] * scale_s, column[3] * scale_t, column[4] * scale_t
        picked = column[5]
    for k, s, t in pairs:
        hit = hits_of(bases_ref[k], position, s.shape)
        weight = jnp.exp(t - top_t)
        mass_s += jnp.sum(jnp.exp(s - top_s), axis=1, keepdims=True)
        mass_t += jnp.sum(weight, axis=1, keepdims=True)
        cross += jnp.sum(weight * (t - s), axis=1, keepdims=True)
        picked += jnp.sum(jnp.where(hit, s, 0.0), axis=1, keepdims=True)
    lane = lax.broadcasted_iota(jnp.int32, (ROWS, stats_ref.shape[1]), 1)
    out = jnp.zeros(lane.shape, F32)
    for k, value in enumerate((top_s, top_t, mass_s, mass_t, cross, picked)):
        out = jnp.where(lane == k, value, out)
    stats_ref[block, :] = out


def forward_kernel(
    spans, quarters, ranks, bases_ref, w_any, codes_ref, hidden_any, position_ref,
    target_head, target_mid, target_tail,
    z_ref, head_any, mid_any, tail_any, stats_ref,
    w_ref, hidden_ref, head_ref, mid_ref, tail_ref, sems, out_sems,
):
    low = quarters + 1
    copies = fetch(w_any, w_ref, sems, spans[:low])
    hidden_copy = pltpu.make_async_copy(hidden_any, hidden_ref, out_sems.at[3])
    hidden_copy.start()
    copies += fetch(w_any, w_ref, sems, spans[low:], first=low)
    rank_mid, rank_tail = ranks
    n_dp, per = 2 * codes_ref.shape[0] // quarters, quarters // 2
    depth = rank_mid // per
    codes = [codes_ref[k].astype(F32) for k in range(codes_ref.shape[0])]
    for q in range(quarters):
        first = q % per * depth
        z_ref[q] = jnp.concatenate(
            [codes[2 * j + q // per][first : first + depth] for j in range(n_dp)], axis=0
        ).astype(BF16)
    z_ref[quarters] = jnp.concatenate(
        [code[rank_mid : rank_mid + rank_tail] for code in codes], axis=0
    ).astype(BF16)

    def weight(k):
        copies[k].wait()
        return w_ref[:, spans[k][0] : spans[k][0] + spans[k][1]]

    outs = [
        pltpu.make_async_copy(ref, out, out_sems.at[k])
        for k, (ref, out) in enumerate(
            ((mid_ref, mid_any), (tail_ref, tail_any), (head_ref, head_any))
        )
    ]
    for q in range(quarters):
        part = dot(z_ref[q], weight(q), 0, 0)
        mid_ref[...] = part if q == 0 else mid_ref[...] + part
    outs[0].start()
    tail_ref[...] = dot(z_ref[quarters], weight(quarters), 0, 0)
    outs[1].start()
    rows = head_ref.shape[0]
    tiers = ((1, mid_ref, target_mid), (2, tail_ref, target_tail))
    row_blocks(
        rows,
        lambda block: add_statistics(bases_ref, tiers, position_ref, stats_ref, block, True),
    )
    hidden_copy.wait()
    for k in range(low, len(spans)):
        part = dot(hidden_ref[k - low], weight(k), 0, 0)
        head_ref[...] = part if k == low else head_ref[...] + part
    outs[2].start()
    tiers_head = ((0, head_ref, target_head),)
    row_blocks(
        rows,
        lambda block: add_statistics(bases_ref, tiers_head, position_ref, stats_ref, block, False),
    )
    for copy in outs:
        copy.wait()


def backward_kernel(
    spans, ranks, bases_ref, w_any, lse_ref, position_ref, s_head, s_mid, s_tail,
    target_head, target_mid, target_tail,
    g_head, g_mid, g_tail, dz_ref, w_ref, sems,
):
    copies = fetch(w_any, w_ref, sems, spans)
    tiers = (
        (s_head, target_head, g_head), (s_mid, target_mid, g_mid), (s_tail, target_tail, g_tail)
    )

    def body(block):
        position, lse = position_ref[block, :], lse_ref[block, :]
        lse_s, lse_t = lse[:, 0:1], lse[:, 1:2]
        for k, (s_ref, t_ref, g_ref) in enumerate(tiers):
            s, t = s_ref[block, :], t_ref[block, :].astype(F32)
            hit = hits_of(bases_ref[k], position, s.shape)
            g = 2.0 * jnp.exp(s - lse_s) - jnp.exp(t - lse_t) - jnp.where(hit, 1.0, 0.0)
            g_ref[block, :] = g.astype(BF16)

    row_blocks(s_head.shape[0], body)
    rank_mid, rank_tail = ranks
    quarters = len(spans) - 1
    n_vocab, padded, rows = dz_ref.shape
    per = quarters // 2
    depth = rank_mid // per
    parts = []
    for q, (start, size) in enumerate(spans):
        copies[q].wait()
        grad = g_tail if q == quarters else g_mid
        parts.append(dot(w_ref[:, start : start + size], grad[...], 1, 1))
    zeros = jnp.zeros((padded - rank_mid - rank_tail, rows), F32)
    for k in range(n_vocab):
        first = k // 2 * depth
        pieces = [parts[k % 2 * per + q][first : first + depth] for q in range(per)]
        pieces += [parts[quarters][k * rank_tail : (k + 1) * rank_tail], zeros]
        dz_ref[k] = jnp.concatenate(pieces, axis=0).astype(BF16)


def weight_grads_kernel(spans, z_ref, mid_ref, tail_ref, out_any, out_ref, sems):
    copies = []
    for q, (start, size) in enumerate(spans):
        grad = tail_ref if q == len(spans) - 1 else mid_ref
        columns = pl.ds(start, size)
        out_ref[:, columns] = dot(z_ref[q], grad[...], 1, 0).astype(BF16)
        copies.append(
            pltpu.make_async_copy(out_ref.at[:, columns], out_any.at[:, columns], sems.at[q])
        )
        copies[-1].start()
    for copy in copies:
        copy.wait()


def hidden_head_kernel(spans, depth, me_ref, w_any, g_ref, out_ref, w_ref, sems):
    copies = fetch(w_any, w_ref, sems, spans, spans[0][0])
    n_out, height, _ = out_ref.shape
    n_dp = w_ref.shape[0] // depth
    per = height // depth
    for half in range(n_out // n_dp):
        parts = []
        for q in range(half * per, (half + 1) * per):
            copies[q].wait()
            start = spans[q][0] - spans[0][0]
            parts.append(dot(w_ref[:, start : start + spans[q][1]], g_ref[...], 1, 1))
        for j in range(n_dp):
            k = j * (n_out // n_dp) + half
            rows = slice(j * depth, (j + 1) * depth)
            head = jnp.concatenate([part[rows] for part in parts], axis=0)
            out_ref[me_ref[0] ^ k] = head.astype(BF16)


def hidden_kernel(
    me_ref, head_ref, proj_ref, dz_ref,
    a_own, a_near, a_lo, a_hi, a_other, b_own, b_near, b_lo, b_hi, b_other,
):
    cut = head_ref.shape[1] // 2
    a_refs = (a_own, a_near, (a_lo, a_hi), a_other)
    b_refs = (b_own, b_near, (b_lo, b_hi), b_other)
    for flip in range(head_ref.shape[0]):
        proj = proj_ref[me_ref[0] ^ flip]
        term = (head_ref[flip].astype(F32) + dot(proj, dz_ref[...], 1, 0)).astype(BF16)
        z, y = flip // 4, flip % 4
        for refs, chunk, k, part in ((a_refs, z, y, term[:cut]), (b_refs, y, z, term[cut:])):
            if chunk == 2:
                refs[2][k // 2][k % 2] = part
            else:
                refs[chunk][k] = part


def fold_kernel(*refs):
    n = len(refs) // 6
    for k in range(n):
        near, hi, other, lo = refs[4 * k : 4 * k + 4]
        near_out, other_out = refs[4 * n + 2 * k : 4 * n + 2 * k + 2]
        cut = lo.shape[0]
        near_out[:cut] = near[:cut]
        near_out[cut:] = (near[cut:].astype(F32) + hi[...].astype(F32)).astype(BF16)
        other_out[:cut] = (other[:cut].astype(F32) + lo[...].astype(F32)).astype(BF16)
        other_out[cut:] = other[cut:]


def total_of(refs):
    return sum(ref[...].astype(F32) for ref in refs)


def turn_kernel(*refs):
    for k in range(2):
        total = total_of(refs[3 * k : 3 * k + 3]).astype(BF16)
        for flip in range(4):
            refs[6 + 4 * k + flip][...] = total[flip]


def end_kernel(*refs):
    total = jnp.concatenate([total_of(refs[:4]), total_of(refs[4:8])], axis=0)
    refs[8][...] = total.astype(BF16)


def fold(*rings, beside):
    operands = []
    for near, lo, hi, other, step in rings:
        lo, hi = swap(lo, "vocab", step), swap(hi, "vocab", 3 * step)
        operands += [near, hi, other, lo]
    operands[1], beside = lax.optimization_barrier((operands[1], beside))
    out = in_vmem(
        fold_kernel,
        tuple(
            jax.ShapeDtypeStruct(ring[k].shape, BF16) for ring in rings for k in (0, 3)
        ),
        *operands,
    )
    return [
        (swap(out[2 * k], "vocab", ring[4]), swap(out[2 * k + 1], "vocab", 3 * ring[4]))
        for k, ring in enumerate(rings)
    ] + [beside]


def ring_sums(a, b, early, dz, middle, late):
    (a_near, a_other), (b_near, b_other), (early, dz) = fold(
        (*a[1:], 4), (*b[1:], 1), beside=(early, dz)
    )
    middle = middle(dz)
    chunk = a[0].shape[1:]
    out = in_vmem(
        turn_kernel,
        (jax.ShapeDtypeStruct(chunk, BF16),) * 8,
        a[0], a_near, a_other, b[0], b_near, b_other,
    )
    moved = [
        part if flip == 0 else swap(part, "vocab", flip * step)
        for step, parts in ((1, out[:4]), (4, out[4:]))
        for flip, part in enumerate(parts)
    ]
    moved[0], middle, late = lax.optimization_barrier((moved[0], middle, late))
    total = in_vmem(
        end_kernel, jax.ShapeDtypeStruct((2 * chunk[0], chunk[1]), BF16), *moved
    )
    return total.T, early, middle, late


def spread_vocab(block):
    size = lax.axis_size("vocab")
    return lax.all_to_all(jnp.broadcast_to(block[None], (size,) + block.shape), "vocab", 0, 0)


def per_device(
    hidden,
    head_weight,
    proj_mid,
    proj_tail,
    mid_weight,
    tail_weight,
    target_head,
    target_mid,
    target_tail,
    top_ids,
    tier_of,
):
    n_vocab = lax.axis_size("vocab")
    n_dp = lax.axis_size("dp")
    v = lax.axis_index("vocab")
    rows, width = hidden.shape
    depth = head_weight.shape[0]
    rank_mid, rank_tail = proj_mid.shape[1], proj_tail.shape[1]
    ranks = rank_mid + rank_tail

    depth_tail = tail_weight.shape[0]
    quarters, groups = mid_weight.shape[0] // depth_tail, depth // depth_tail
    widths = (head_weight.shape[1], mid_weight.shape[1], tail_weight.shape[1])
    spans = column_spans((quarters, 1, groups), (widths[1], widths[2], widths[0]))
    low, head_spans = spans[: quarters + 1], spans[quarters + 1 :]
    packed_width = spans[-1][0] + spans[-1][1]
    low_width = head_spans[0][0]
    height = n_dp * depth_tail
    vmem, smem, anywhere = (
        pl.BlockSpec(memory_space=space) for space in (pltpu.VMEM, pltpu.SMEM, pl.ANY)
    )

    def shaped(*shape, dtype=BF16):
        return jax.ShapeDtypeStruct(shape, dtype)

    with jax.named_scope("gather_weights"):
        packed = in_vmem(
            functools.partial(pack_kernel, spans, quarters),
            shaped(depth_tail, packed_width),
            mid_weight,
            tail_weight,
            head_weight,
            mib=60,
        )
        weights = lax.all_gather(packed, "dp", axis=0, tiled=True)
    with jax.named_scope("gather_proj"):
        packed, proj_mid, proj_tail = lax.optimization_barrier((packed, proj_mid, proj_tail))
        pad = -ranks % 16
        proj_t = jnp.concatenate(
            [proj_mid.T, proj_tail.T, jnp.zeros((pad, depth), BF16)], axis=0
        )
        proj_full = gather_dp(proj_t, 1, (ranks + pad) // 32 * 16)
    with jax.named_scope("codes"):
        codes = dot(proj_full, hidden, 1, 1).astype(BF16)
    with jax.named_scope("spread_codes"):
        codes_all = spread_vocab(codes)
    with jax.named_scope("spread_hidden"):
        piece = rows // n_vocab
        mine = lax.dynamic_slice_in_dim(hidden, v * piece, piece, 0)
        mine = mine.reshape(piece, n_dp, depth).transpose(1, 0, 2)
        mine = lax.all_to_all(mine, "dp", 0, 0)
        mine, codes_all = lax.optimization_barrier((mine, codes_all))
        x_all = lax.all_gather(mine.reshape(n_dp * piece, depth), "vocab", axis=0)
    with jax.named_scope("arrange"):
        hidden_t = hidden.T.reshape(n_dp, groups, depth_tail, rows).transpose(1, 0, 2, 3)
        hidden_t = hidden_t.reshape(groups, height, rows)
        proj_rows = proj_full.T.reshape(n_vocab, width // n_vocab, ranks + pad)
        starts = (0, widths[0] * n_vocab, (widths[0] + widths[1]) * n_vocab)
        bases = jnp.stack([start + v * w for start, w in zip(starts, widths)]).astype(jnp.int32)
        positions = jnp.take(tier_of, top_ids).astype(jnp.int32)[:, None]
        codes_all, hidden_t, proj_rows, positions = lax.optimization_barrier(
            (codes_all, hidden_t, proj_rows, positions)
        )

    with jax.named_scope("logits"):
        z, s_head, s_mid, s_tail, stats = in_vmem(
            functools.partial(forward_kernel, spans, quarters, (rank_mid, rank_tail)),
            (
                shaped(quarters + 1, height, rows),
                shaped(rows, widths[0], dtype=F32),
                shaped(rows, widths[1], dtype=F32),
                shaped(rows, widths[2], dtype=F32),
                shaped(rows, 128, dtype=F32),
            ),
            bases,
            weights,
            codes_all,
            hidden_t,
            positions,
            target_head,
            target_mid,
            target_tail,
            in_specs=[smem, anywhere, vmem, anywhere] + [vmem] * 4,
            out_specs=(vmem, anywhere, anywhere, anywhere, vmem),
            scratch_shapes=[
                pltpu.VMEM((height, packed_width), BF16),
                pltpu.VMEM(hidden_t.shape, BF16),
                pltpu.VMEM((rows, widths[0]), F32),
                pltpu.VMEM((rows, widths[1]), F32),
                pltpu.VMEM((rows, widths[2]), F32),
                pltpu.SemaphoreType.DMA((len(spans),)),
                pltpu.SemaphoreType.DMA((4,)),
            ],
            mib=60,
        )
    with jax.named_scope("spread_statistics"):
        stats = spread_vocab(stats[:, :8].T)
        near_s, near_t, mass_s, mass_t, cross, picked = (stats[:, k] for k in range(6))
        top_s, top_t = jnp.max(near_s, axis=0), jnp.max(near_t, axis=0)
        scale_s, scale_t = jnp.exp(near_s - top_s[None]), jnp.exp(near_t - top_t[None])
        mass_s = jnp.sum(mass_s * scale_s, axis=0)
        mass_t = jnp.sum(mass_t * scale_t, axis=0)
        cross = jnp.sum(cross * scale_t, axis=0)
        picked = jnp.sum(picked, axis=0)
        lse_s = top_s + jnp.log(mass_s)
        lse_t = top_t + jnp.log(mass_t)
        row_loss = cross / mass_t - lse_t + 2.0 * lse_s - picked
        lse = jnp.stack([lse_s, lse_t], axis=1)
    with jax.named_scope("grad_logits"):
        g_head, g_mid, g_tail, dz = in_vmem(
            functools.partial(backward_kernel, low, (rank_mid, rank_tail)),
            (
                shaped(rows, widths[0]),
                shaped(rows, widths[1]),
                shaped(rows, widths[2]),
                shaped(n_vocab, ranks + pad, rows),
            ),
            bases,
            weights,
            lse,
            positions,
            s_head,
            s_mid,
            s_tail,
            target_head,
            target_mid,
            target_tail,
            in_specs=[smem, anywhere] + [vmem] * 8,
            scratch_shapes=[
                pltpu.VMEM((height, low_width), BF16),
                pltpu.SemaphoreType.DMA((len(low),)),
            ],
            mib=48,
        )
        x_all = x_all.reshape(n_dp * rows, depth)
    with jax.named_scope("hidden_head"):
        me = v.astype(jnp.int32).reshape(1)
        cut = width // n_vocab // 2
        head_term = in_vmem(
            functools.partial(hidden_head_kernel, head_spans, depth_tail),
            shaped(n_vocab, 2 * cut, rows),
            me,
            weights,
            g_head,
            in_specs=[smem, anywhere, vmem],
            scratch_shapes=[
                pltpu.VMEM((height, packed_width - low_width), BF16),
                pltpu.SemaphoreType.DMA((len(head_spans),)),
            ],
            mib=48,
        )
    with jax.named_scope("head_grad"):
        g_rows = g_head.reshape(n_vocab, piece, -1)
        g_near, g_other = ring_near(g_rows, "dp", 2)
        g_near, g_other, head_term = lax.optimization_barrier((g_near, g_other, head_term))
        g_far = ring_far(g_near, g_other, "dp", 2, n_vocab // 2)
        g_all = both_cores([g_rows, g_near, g_far, g_other], 1)
        g_all = g_all.reshape(n_dp * rows, -1)
    with jax.named_scope("code_grads"):
        dz = lax.all_to_all(dz, "vocab", 0, 0)
        dz = jnp.sum(dz.astype(F32), axis=0).astype(BF16)
        dz, g_all, x_all = lax.optimization_barrier((dz, g_all, x_all))
    with jax.named_scope("mid_tail_grads"):
        packed_grad = in_vmem(
            functools.partial(weight_grads_kernel, low),
            shaped(height, low_width),
            z,
            g_mid,
            g_tail,
            out_specs=anywhere,
            scratch_shapes=[
                pltpu.VMEM((height, low_width), BF16),
                pltpu.SemaphoreType.DMA((len(low),)),
            ],
            mib=48,
        )
        packed_grad = lax.psum_scatter(packed_grad, "dp", scatter_dimension=0, tiled=True)
        mid_grad, tail_grad = in_vmem(
            functools.partial(unpack_kernel, low),
            (shaped(*mid_weight.shape), shaped(*tail_weight.shape)),
            packed_grad,
        )
    with jax.named_scope("hidden_grad"):
        chunks = [shaped(4, cut, rows)] * 2 + [shaped(2, cut, rows)] * 2 + [shaped(4, cut, rows)]
        pieces = in_vmem(
            hidden_kernel,
            tuple(chunks * 2),
            me,
            head_term,
            proj_rows,
            dz,
            in_specs=[smem] + [vmem] * 3,
            mib=48,
        )
    with jax.named_scope("head_proj_grads"):
        head_grad = dot(x_all, g_all, 0, 0).astype(BF16)

    def proj_grads(dz):
        with jax.named_scope("head_proj_grads"):
            dz_all = jnp.broadcast_to(dz.T[None], (n_dp, rows, ranks + pad))
            dz_all = lax.all_to_all(dz_all, "dp", 0, 0).reshape(n_dp, n_vocab, piece, -1)
            dz_all = dz_all.transpose(1, 0, 2, 3).reshape(n_dp * rows, -1)
            return dot(dz_all, x_all, 0, 0).astype(BF16)

    with jax.named_scope("hidden_grad_sum"):
        hidden_grad, head_grad, proj_grad, (mid_grad, tail_grad) = ring_sums(
            pieces[:5], pieces[5:], head_grad, dz, proj_grads, (mid_grad, tail_grad)
        )
    return (
        head_grad,
        proj_grad[:rank_mid].T,
        proj_grad[rank_mid:ranks].T,
        mid_grad,
        tail_grad,
        hidden_grad,
        row_loss,
    )


def solution(mesh):
    split = P("dp", "vocab")
    in_specs = (P("dp", None),) + (split,) * 8 + (P("dp"), P())
    out_specs = (split,) * 6 + (P("dp"),)
    return jax.shard_map(
        per_device, mesh=mesh, in_specs=in_specs, out_specs=out_specs, check_vma=False
    )
```

```python
import functools

import jax
import jax.numpy as jnp
from jax import lax
from jax.experimental import pallas as pl
from jax.experimental.pallas import tpu as pltpu
from jax.sharding import PartitionSpec as P

BF16 = jnp.bfloat16
F32 = jnp.float32


def dot(left, right, left_dim, right_dim):
    return lax.dot_general(
        left, right, (((left_dim,), (right_dim,)), ((), ())), preferred_element_type=F32
    )


def swap(block, axis_name, flip):
    pairs = [(i, i ^ flip) for i in range(lax.axis_size(axis_name))]
    return lax.ppermute(block, axis_name, pairs)


def ring_near(block, axis_name, step):
    return swap(block, axis_name, step), swap(block, axis_name, 3 * step)


def ring_far(near, other, axis_name, step, half):
    return jnp.concatenate(
        [swap(other[:half], axis_name, step), swap(near[half:], axis_name, 3 * step)], axis=0
    )


def place_kernel(axis, spots_ref, *refs):
    blocks, out, sems = refs[:-2], refs[-2], refs[-1]
    copies = []
    for k, block in enumerate(blocks):
        size = block.shape[axis]
        start = pl.multiple_of(spots_ref[k] * size, size)
        spot = out.at[(slice(None),) * axis + (pl.ds(start, size),)]
        copies.append(pltpu.make_async_copy(block, spot, sems.at[k]))
    for copy in copies:
        copy.start()
    for copy in copies:
        copy.wait()


def place(blocks, spots, axis):
    shape = list(blocks[0].shape)
    shape[axis] *= len(blocks)
    moved = 2 * len(blocks) * blocks[0].size * blocks[0].dtype.itemsize
    return pl.pallas_call(
        functools.partial(place_kernel, axis),
        out_shape=jax.ShapeDtypeStruct(tuple(shape), blocks[0].dtype),
        in_specs=[pl.BlockSpec(memory_space=pltpu.SMEM)]
        + [pl.BlockSpec(memory_space=pltpu.VMEM)] * len(blocks),
        out_specs=pl.BlockSpec(memory_space=pl.ANY),
        scratch_shapes=[pltpu.SemaphoreType.DMA((len(blocks),))],
        compiler_params=pltpu.CompilerParams(vmem_limit_bytes=16 << 20),
        cost_estimate=pl.CostEstimate(flops=0, bytes_accessed=moved, transcendentals=0),
    )(jnp.stack(spots).astype(jnp.int32), *blocks)


def both_cores(parts, axis):
    blocks = [p for part in parts for p in (part, swap(part, "dp", 1))]
    me = lax.axis_index("dp")
    return place(blocks, [me ^ flip for flip in range(len(blocks))], axis)


def gather_dp(block, axis, half):
    near, other = ring_near(block, "dp", 2)
    far = ring_far(near, other, "dp", 2, half)
    return both_cores([block, near, far, other], axis)


def in_vmem(kernel, out_shape, *operands, in_specs=None, out_specs=None, scratch_shapes=(), mib=16):
    outs = out_shape if isinstance(out_shape, tuple) else (out_shape,)
    size = sum(a.size * a.dtype.itemsize for a in operands + outs)
    specs = in_specs or [pl.BlockSpec(memory_space=pltpu.VMEM)] * len(operands)
    return pl.pallas_call(
        kernel,
        out_shape=out_shape,
        in_specs=specs,
        out_specs=out_specs or jax.tree.map(lambda _: pl.BlockSpec(memory_space=pltpu.VMEM), out_shape),
        scratch_shapes=scratch_shapes,
        compiler_params=pltpu.CompilerParams(vmem_limit_bytes=mib << 20),
        cost_estimate=pl.CostEstimate(flops=2 * 10**9, bytes_accessed=size, transcendentals=0),
    )(*operands)


def fetch(source, held, sems, spans, base=0, first=0):
    copies = [
        pltpu.make_async_copy(
            source.at[:, pl.ds(start, size)], held.at[:, pl.ds(start - base, size)], sems.at[first + k]
        )
        for k, (start, size) in enumerate(spans)
    ]
    for copy in copies:
        copy.start()
    return copies


def column_spans(groups, widths):
    spans, start = [], 0
    for count, width in zip(groups, widths):
        for _ in range(count):
            spans.append((start, width))
            start += width
    return spans


def pack_kernel(spans, quarters, mid_ref, tail_ref, head_ref, out_ref):
    depth = tail_ref.shape[0]
    mid, head = mid_ref[...].astype(F32), head_ref[...].astype(F32)
    for k, (start, size) in enumerate(spans):
        if k < quarters:
            piece = mid[k * depth : (k + 1) * depth].astype(BF16)
        elif k == quarters:
            piece = tail_ref[...]
        else:
            row = (k - quarters - 1) * depth
            piece = head[row : row + depth].astype(BF16)
        out_ref[:, start : start + size] = piece


def unpack_kernel(spans, packed_ref, mid_ref, tail_ref):
    quarters = [packed_ref[:, a : a + size].astype(F32) for a, size in spans[:-1]]
    mid_ref[...] = jnp.concatenate(quarters, axis=0).astype(BF16)
    start, size = spans[-1]
    tail_ref[...] = packed_ref[:, start : start + size]


ROWS = 32
UNROLL = 2


def row_blocks(rows, body):
    def step(k, carry):
        body(pl.ds(pl.multiple_of(k * ROWS, ROWS), ROWS))
        return carry

    lax.fori_loop(0, rows // ROWS, step, 0, unroll=UNROLL)


def hits_of(base, position, shape):
    return position - base == lax.broadcasted_iota(jnp.int32, shape, 1)


def add_statistics(bases_ref, tiers, position_ref, stats_ref, block, first):
    pairs = [(k, s[block, :], t[block, :].astype(F32)) for k, s, t in tiers]
    position = position_ref[block, :]
    old = stats_ref[block, :]
    column = [old[:, k : k + 1] for k in range(6)]
    top_s, top_t = (None, None) if first else column[:2]
    for _, s, t in pairs:
        here_s, here_t = (jnp.max(a, axis=1, keepdims=True) for a in (s, t))
        top_s = here_s if top_s is None else jnp.maximum(top_s, here_s)
        top_t = here_t if top_t is None else jnp.maximum(top_t, here_t)
    if first:
        mass_s = mass_t = cross = picked = jnp.zeros_like(top_s)
    else:
        scale_s, scale_t = jnp.exp(column[0] - top_s), jnp.exp(column[1] - top_t)
        mass_s, mass_t, cross = column[2] * scale_s, column[3] * scale_t, column[4] * scale_t
        picked = column[5]
    for k, s, t in pairs:
        hit = hits_of(bases_ref[k], position, s.shape)
        weight = jnp.exp(t - top_t)
        mass_s += jnp.sum(jnp.exp(s - top_s), axis=1, keepdims=True)
        mass_t += jnp.sum(weight, axis=1, keepdims=True)
        cross += jnp.sum(weight * (t - s), axis=1, keepdims=True)
        picked += jnp.sum(jnp.where(hit, s, 0.0), axis=1, keepdims=True)
    lane = lax.broadcasted_iota(jnp.int32, (ROWS, stats_ref.shape[1]), 1)
    out = jnp.zeros(lane.shape, F32)
    for k, value in enumerate((top_s, top_t, mass_s, mass_t, cross, picked)):
        out = jnp.where(lane == k, value, out)
    stats_ref[block, :] = out


def forward_kernel(
    spans, quarters, ranks, bases_ref, w_any, codes_ref, hidden_any, position_ref,
    target_head, target_mid, target_tail,
    z_ref, head_any, mid_any, tail_any, stats_ref,
    w_ref, hidden_ref, head_ref, mid_ref, tail_ref, sems, out_sems,
):
    low = quarters + 1
    copies = fetch(w_any, w_ref, sems, spans[:low])
    hidden_copy = pltpu.make_async_copy(hidden_any, hidden_ref, out_sems.at[3])
    hidden_copy.start()
    copies += fetch(w_any, w_ref, sems, spans[low:], first=low)
    rank_mid, rank_tail = ranks
    n_dp, per = 2 * codes_ref.shape[0] // quarters, quarters // 2
    depth = rank_mid // per
    codes = [codes_ref[k].astype(F32) for k in range(codes_ref.shape[0])]
    for q in range(quarters):
        first = q % per * depth
        z_ref[q] = jnp.concatenate(
            [codes[2 * j + q // per][first : first + depth] for j in range(n_dp)], axis=0
        ).astype(BF16)
    z_ref[quarters] = jnp.concatenate(
        [code[rank_mid : rank_mid + rank_tail] for code in codes], axis=0
    ).astype(BF16)

    def weight(k):
        copies[k].wait()
        return w_ref[:, spans[k][0] : spans[k][0] + spans[k][1]]

    outs = [
        pltpu.make_async_copy(ref, out, out_sems.at[k])
        for k, (ref, out) in enumerate(
            ((mid_ref, mid_any), (tail_ref, tail_any), (head_ref, head_any))
        )
    ]
    for q in range(quarters):
        part = dot(z_ref[q], weight(q), 0, 0)
        mid_ref[...] = part if q == 0 else mid_ref[...] + part
    outs[0].start()
    tail_ref[...] = dot(z_ref[quarters], weight(quarters), 0, 0)
    outs[1].start()
    rows = head_ref.shape[0]
    tiers = ((1, mid_ref, target_mid), (2, tail_ref, target_tail))
    row_blocks(
        rows,
        lambda block: add_statistics(bases_ref, tiers, position_ref, stats_ref, block, True),
    )
    hidden_copy.wait()
    for k in range(low, len(spans)):
        part = dot(hidden_ref[k - low], weight(k), 0, 0)
        head_ref[...] = part if k == low else head_ref[...] + part
    outs[2].start()
    tiers_head = ((0, head_ref, target_head),)
    row_blocks(
        rows,
        lambda block: add_statistics(bases_ref, tiers_head, position_ref, stats_ref, block, False),
    )
    for copy in outs:
        copy.wait()


def backward_kernel(
    spans, ranks, bases_ref, w_any, lse_ref, position_ref, s_head, s_mid, s_tail,
    target_head, target_mid, target_tail,
    g_head, g_mid, g_tail, dz_ref, w_ref, sems,
):
    copies = fetch(w_any, w_ref, sems, spans)
    tiers = (
        (s_head, target_head, g_head), (s_mid, target_mid, g_mid), (s_tail, target_tail, g_tail)
    )

    def body(block):
        position, lse = position_ref[block, :], lse_ref[block, :]
        lse_s, lse_t = lse[:, 0:1], lse[:, 1:2]
        for k, (s_ref, t_ref, g_ref) in enumerate(tiers):
            s, t = s_ref[block, :], t_ref[block, :].astype(F32)
            hit = hits_of(bases_ref[k], position, s.shape)
            g = 2.0 * jnp.exp(s - lse_s) - jnp.exp(t - lse_t) - jnp.where(hit, 1.0, 0.0)
            g_ref[block, :] = g.astype(BF16)

    row_blocks(s_head.shape[0], body)
    rank_mid, rank_tail = ranks
    quarters = len(spans) - 1
    n_vocab, padded, rows = dz_ref.shape
    per = quarters // 2
    depth = rank_mid // per
    parts = []
    for q, (start, size) in enumerate(spans):
        copies[q].wait()
        grad = g_tail if q == quarters else g_mid
        parts.append(dot(w_ref[:, start : start + size], grad[...], 1, 1))
    zeros = jnp.zeros((padded - rank_mid - rank_tail, rows), F32)
    for k in range(n_vocab):
        first = k // 2 * depth
        pieces = [parts[k % 2 * per + q][first : first + depth] for q in range(per)]
        pieces += [parts[quarters][k * rank_tail : (k + 1) * rank_tail], zeros]
        dz_ref[k] = jnp.concatenate(pieces, axis=0).astype(BF16)


def weight_grads_kernel(spans, z_ref, mid_ref, tail_ref, out_any, out_ref, sems):
    copies = []
    for q, (start, size) in enumerate(spans):
        grad = tail_ref if q == len(spans) - 1 else mid_ref
        columns = pl.ds(start, size)
        out_ref[:, columns] = dot(z_ref[q], grad[...], 1, 0).astype(BF16)
        copies.append(
            pltpu.make_async_copy(out_ref.at[:, columns], out_any.at[:, columns], sems.at[q])
        )
        copies[-1].start()
    for copy in copies:
        copy.wait()


def hidden_head_kernel(spans, depth, me_ref, w_any, g_ref, out_ref, w_ref, sems):
    copies = fetch(w_any, w_ref, sems, spans, spans[0][0])
    n_out, height, _ = out_ref.shape
    n_dp = w_ref.shape[0] // depth
    per = height // depth
    for half in range(n_out // n_dp):
        parts = []
        for q in range(half * per, (half + 1) * per):
            copies[q].wait()
            start = spans[q][0] - spans[0][0]
            parts.append(dot(w_ref[:, start : start + spans[q][1]], g_ref[...], 1, 1))
        for j in range(n_dp):
            k = j * (n_out // n_dp) + half
            rows = slice(j * depth, (j + 1) * depth)
            head = jnp.concatenate([part[rows] for part in parts], axis=0)
            out_ref[me_ref[0] ^ k] = head.astype(BF16)


def hidden_kernel(
    me_ref, head_ref, proj_ref, dz_ref,
    a_own, a_near, a_lo, a_hi, a_other, b_own, b_near, b_lo, b_hi, b_other,
):
    cut = head_ref.shape[1] // 2
    a_refs = (a_own, a_near, (a_lo, a_hi), a_other)
    b_refs = (b_own, b_near, (b_lo, b_hi), b_other)
    for flip in range(head_ref.shape[0]):
        proj = proj_ref[me_ref[0] ^ flip]
        term = (head_ref[flip].astype(F32) + dot(proj, dz_ref[...], 1, 0)).astype(BF16)
        z, y = flip // 4, flip % 4
        for refs, chunk, k, part in ((a_refs, z, y, term[:cut]), (b_refs, y, z, term[cut:])):
            if chunk == 2:
                refs[2][k // 2][k % 2] = part
            else:
                refs[chunk][k] = part


def fold_kernel(*refs):
    n = len(refs) // 6
    for k in range(n):
        near, hi, other, lo = refs[4 * k : 4 * k + 4]
        near_out, other_out = refs[4 * n + 2 * k : 4 * n + 2 * k + 2]
        cut = lo.shape[0]
        near_out[:cut] = near[:cut]
        near_out[cut:] = (near[cut:].astype(F32) + hi[...].astype(F32)).astype(BF16)
        other_out[:cut] = (other[:cut].astype(F32) + lo[...].astype(F32)).astype(BF16)
        other_out[cut:] = other[cut:]


def total_of(refs):
    return sum(ref[...].astype(F32) for ref in refs)


def turn_kernel(*refs):
    for k in range(2):
        total = total_of(refs[3 * k : 3 * k + 3]).astype(BF16)
        for flip in range(4):
            refs[6 + 4 * k + flip][...] = total[flip]


def end_kernel(*refs):
    total = jnp.concatenate([total_of(refs[:4]), total_of(refs[4:8])], axis=0)
    refs[8][...] = total.astype(BF16)


def fold(*rings, beside):
    operands = []
    for near, lo, hi, other, step in rings:
        lo, hi = swap(lo, "vocab", step), swap(hi, "vocab", 3 * step)
        operands += [near, hi, other, lo]
    operands[1], beside = lax.optimization_barrier((operands[1], beside))
    out = in_vmem(
        fold_kernel,
        tuple(
            jax.ShapeDtypeStruct(ring[k].shape, BF16) for ring in rings for k in (0, 3)
        ),
        *operands,
    )
    return [
        (swap(out[2 * k], "vocab", ring[4]), swap(out[2 * k + 1], "vocab", 3 * ring[4]))
        for k, ring in enumerate(rings)
    ] + [beside]


def ring_sums(a, b, early, dz, middle, late):
    (a_near, a_other), (b_near, b_other), (early, dz) = fold(
        (*a[1:], 4), (*b[1:], 1), beside=(early, dz)
    )
    middle = middle(dz)
    chunk = a[0].shape[1:]
    out = in_vmem(
        turn_kernel,
        (jax.ShapeDtypeStruct(chunk, BF16),) * 8,
        a[0], a_near, a_other, b[0], b_near, b_other,
    )
    moved = [
        part if flip == 0 else swap(part, "vocab", flip * step)
        for step, parts in ((1, out[:4]), (4, out[4:]))
        for flip, part in enumerate(parts)
    ]
    moved[0], middle, late = lax.optimization_barrier((moved[0], middle, late))
    total = in_vmem(
        end_kernel, jax.ShapeDtypeStruct((2 * chunk[0], chunk[1]), BF16), *moved
    )
    return total.T, early, middle, late


def spread_vocab(block):
    size = lax.axis_size("vocab")
    return lax.all_to_all(jnp.broadcast_to(block[None], (size,) + block.shape), "vocab", 0, 0)


def per_device(
    hidden,
    head_weight,
    proj_mid,
    proj_tail,
    mid_weight,
    tail_weight,
    target_head,
    target_mid,
    target_tail,
    top_ids,
    tier_of,
):
    n_vocab = lax.axis_size("vocab")
    n_dp = lax.axis_size("dp")
    v = lax.axis_index("vocab")
    rows, width = hidden.shape
    depth = head_weight.shape[0]
    rank_mid, rank_tail = proj_mid.shape[1], proj_tail.shape[1]
    ranks = rank_mid + rank_tail

    depth_tail = tail_weight.shape[0]
    quarters, groups = mid_weight.shape[0] // depth_tail, depth // depth_tail
    widths = (head_weight.shape[1], mid_weight.shape[1], tail_weight.shape[1])
    spans = column_spans((quarters, 1, groups), (widths[1], widths[2], widths[0]))
    low, head_spans = spans[: quarters + 1], spans[quarters + 1 :]
    packed_width = spans[-1][0] + spans[-1][1]
    low_width = head_spans[0][0]
    height = n_dp * depth_tail
    vmem, smem, anywhere = (
        pl.BlockSpec(memory_space=space) for space in (pltpu.VMEM, pltpu.SMEM, pl.ANY)
    )

    def shaped(*shape, dtype=BF16):
        return jax.ShapeDtypeStruct(shape, dtype)

    with jax.named_scope("gather_weights"):
        packed = in_vmem(
            functools.partial(pack_kernel, spans, quarters),
            shaped(depth_tail, packed_width),
            mid_weight,
            tail_weight,
            head_weight,
            mib=60,
        )
        weights = lax.all_gather(packed, "dp", axis=0, tiled=True)
    with jax.named_scope("gather_proj"):
        packed, proj_mid, proj_tail = lax.optimization_barrier((packed, proj_mid, proj_tail))
        pad = -ranks % 16
        proj_t = jnp.concatenate(
            [proj_mid.T, proj_tail.T, jnp.zeros((pad, depth), BF16)], axis=0
        )
        proj_full = gather_dp(proj_t, 1, (ranks + pad) // 32 * 16)
    with jax.named_scope("codes"):
        codes = dot(proj_full, hidden, 1, 1).astype(BF16)
    with jax.named_scope("spread_codes"):
        codes_all = spread_vocab(codes)
    with jax.named_scope("spread_hidden"):
        piece = rows // n_vocab
        mine = lax.dynamic_slice_in_dim(hidden, v * piece, piece, 0)
        mine = mine.reshape(piece, n_dp, depth).transpose(1, 0, 2)
        mine = lax.all_to_all(mine, "dp", 0, 0)
        mine, codes_all = lax.optimization_barrier((mine, codes_all))
        x_all = lax.all_gather(mine.reshape(n_dp * piece, depth), "vocab", axis=0)
    with jax.named_scope("arrange"):
        hidden_t = hidden.T.reshape(n_dp, groups, depth_tail, rows).transpose(1, 0, 2, 3)
        hidden_t = hidden_t.reshape(groups, height, rows)
        proj_rows = proj_full.T.reshape(n_vocab, width // n_vocab, ranks + pad)
        starts = (0, widths[0] * n_vocab, (widths[0] + widths[1]) * n_vocab)
        bases = jnp.stack([start + v * w for start, w in zip(starts, widths)]).astype(jnp.int32)
        positions = jnp.take(tier_of, top_ids).astype(jnp.int32)[:, None]
        codes_all, hidden_t, proj_rows, positions = lax.optimization_barrier(
            (codes_all, hidden_t, proj_rows, positions)
        )

    with jax.named_scope("logits"):
        z, s_head, s_mid, s_tail, stats = in_vmem(
            functools.partial(forward_kernel, spans, quarters, (rank_mid, rank_tail)),
            (
                shaped(quarters + 1, height, rows),
                shaped(rows, widths[0], dtype=F32),
                shaped(rows, widths[1], dtype=F32),
                shaped(rows, widths[2], dtype=F32),
                shaped(rows, 128, dtype=F32),
            ),
            bases,
            weights,
            codes_all,
            hidden_t,
            positions,
            target_head,
            target_mid,
            target_tail,
            in_specs=[smem, anywhere, vmem, anywhere] + [vmem] * 4,
            out_specs=(vmem, anywhere, anywhere, anywhere, vmem),
            scratch_shapes=[
                pltpu.VMEM((height, packed_width), BF16),
                pltpu.VMEM(hidden_t.shape, BF16),
                pltpu.VMEM((rows, widths[0]), F32),
                pltpu.VMEM((rows, widths[1]), F32),
                pltpu.VMEM((rows, widths[2]), F32),
                pltpu.SemaphoreType.DMA((len(spans),)),
                pltpu.SemaphoreType.DMA((4,)),
            ],
            mib=60,
        )
    with jax.named_scope("spread_statistics"):
        stats = spread_vocab(stats[:, :8].T)
        near_s, near_t, mass_s, mass_t, cross, picked = (stats[:, k] for k in range(6))
        top_s, top_t = jnp.max(near_s, axis=0), jnp.max(near_t, axis=0)
        scale_s, scale_t = jnp.exp(near_s - top_s[None]), jnp.exp(near_t - top_t[None])
        mass_s = jnp.sum(mass_s * scale_s, axis=0)
        mass_t = jnp.sum(mass_t * scale_t, axis=0)
        cross = jnp.sum(cross * scale_t, axis=0)
        picked = jnp.sum(picked, axis=0)
        lse_s = top_s + jnp.log(mass_s)
        lse_t = top_t + jnp.log(mass_t)
        row_loss = cross / mass_t - lse_t + 2.0 * lse_s - picked
        lse = jnp.stack([lse_s, lse_t], axis=1)
    with jax.named_scope("grad_logits"):
        g_head, g_mid, g_tail, dz = in_vmem(
            functools.partial(backward_kernel, low, (rank_mid, rank_tail)),
            (
                shaped(rows, widths[0]),
                shaped(rows, widths[1]),
                shaped(rows, widths[2]),
                shaped(n_vocab, ranks + pad, rows),
            ),
            bases,
            weights,
            lse,
            positions,
            s_head,
            s_mid,
            s_tail,
            target_head,
            target_mid,
            target_tail,
            in_specs=[smem, anywhere] + [vmem] * 8,
            scratch_shapes=[
                pltpu.VMEM((height, low_width), BF16),
                pltpu.SemaphoreType.DMA((len(low),)),
            ],
            mib=48,
        )
        x_all = x_all.reshape(n_dp * rows, depth)
    with jax.named_scope("hidden_head"):
        me = v.astype(jnp.int32).reshape(1)
        cut = width // n_vocab // 2
        head_term = in_vmem(
            functools.partial(hidden_head_kernel, head_spans, depth_tail),
            shaped(n_vocab, 2 * cut, rows),
            me,
            weights,
            g_head,
            in_specs=[smem, anywhere, vmem],
            scratch_shapes=[
                pltpu.VMEM((height, packed_width - low_width), BF16),
                pltpu.SemaphoreType.DMA((len(head_spans),)),
            ],
            mib=48,
        )
    with jax.named_scope("head_grad"):
        g_rows = g_head.reshape(n_vocab, piece, -1)
        g_near, g_other = ring_near(g_rows, "dp", 2)
        g_near, g_other, head_term = lax.optimization_barrier((g_near, g_other, head_term))
        g_far = ring_far(g_near, g_other, "dp", 2, n_vocab // 2)
    with jax.named_scope("code_grads"):
        dz = lax.all_to_all(dz, "vocab", 0, 0)
        dz = jnp.sum(dz.astype(F32), axis=0).astype(BF16)
        dz, g_far, x_all = lax.optimization_barrier((dz, g_far, x_all))
    with jax.named_scope("mid_tail_grads"):
        packed_grad = in_vmem(
            functools.partial(weight_grads_kernel, low),
            shaped(height, low_width),
            z,
            g_mid,
            g_tail,
            out_specs=anywhere,
            scratch_shapes=[
                pltpu.VMEM((height, low_width), BF16),
                pltpu.SemaphoreType.DMA((len(low),)),
            ],
            mib=48,
        )
        packed_grad = lax.psum_scatter(packed_grad, "dp", scatter_dimension=0, tiled=True)
        mid_grad, tail_grad = in_vmem(
            functools.partial(unpack_kernel, low),
            (shaped(*mid_weight.shape), shaped(*tail_weight.shape)),
            packed_grad,
        )
    with jax.named_scope("hidden_grad"):
        chunks = [shaped(4, cut, rows)] * 2 + [shaped(2, cut, rows)] * 2 + [shaped(4, cut, rows)]
        pieces = in_vmem(
            hidden_kernel,
            tuple(chunks * 2),
            me,
            head_term,
            proj_rows,
            dz,
            in_specs=[smem] + [vmem] * 3,
            mib=48,
        )
    with jax.named_scope("head_proj_grads"):
        g_all = both_cores([g_rows, g_near, g_far, g_other], 1)
        g_all = g_all.reshape(n_dp * rows, -1)
        head_grad = dot(x_all, g_all, 0, 0).astype(BF16)

    def proj_grads(dz):
        with jax.named_scope("head_proj_grads"):
            dz_all = jnp.broadcast_to(dz.T[None], (n_dp, rows, ranks + pad))
            dz_all = lax.all_to_all(dz_all, "dp", 0, 0).reshape(n_dp, n_vocab, piece, -1)
            dz_all = dz_all.transpose(1, 0, 2, 3).reshape(n_dp * rows, -1)
            return dot(dz_all, x_all, 0, 0).astype(BF16)

    with jax.named_scope("hidden_grad_sum"):
        hidden_grad, head_grad, proj_grad, (mid_grad, tail_grad) = ring_sums(
            pieces[:5], pieces[5:], head_grad, dz, proj_grads, (mid_grad, tail_grad)
        )
    return (
        head_grad,
        proj_grad[:rank_mid].T,
        proj_grad[rank_mid:ranks].T,
        mid_grad,
        tail_grad,
        hidden_grad,
        row_loss,
    )


def solution(mesh):
    split = P("dp", "vocab")
    in_specs = (P("dp", None),) + (split,) * 8 + (P("dp"), P())
    out_specs = (split,) * 6 + (P("dp"),)
    return jax.shard_map(
        per_device, mesh=mesh, in_specs=in_specs, out_specs=out_specs, check_vma=False
    )
```
